256 devices in a mesh: ctx: 32 (over y, x, core), pipe: 8 (over z).
Axes of the slice: x: 4, y: 4, z: 8, core: 2. Of those that a mesh axis runs over, the one named last changes fastest.
Arguments:
- tokens: bfloat16 [1, 4096, 2048], P(None, 'ctx'), may hold values from -6 to 6
- w_qkv: bfloat16 [8, 16, 128, 384], P('pipe'), may hold values from -0.5 to 0.5
- norm_gain: float32 [8, 2048], P('pipe'), may hold values from 0.5 to 1.5
- out_gain: float32 [8, 2048], P('pipe'), may hold values from 0.5 to 1.5
Outputs:
- hidden: bfloat16 [8, 1, 4096, 2048], P('pipe', None, 'ctx')
The draws below stay inside these ranges and needn't reach their ends.
All inputs are finite; a program needn't handle non-finite values.
Results may differ from the reference program's by a relative error of at most 0.03.
Values may be sent and summed in bfloat16 or wider, within the bound.
No kernel may reach another device: no remote copies, remote signals or barrier semaphores. Data moves between devices by JAX's collectives and lax.ppermute only.
A program may use at most 128 MiB of HBM per device.

```python
import jax
import jax.numpy as jnp
from jax import lax

HEADS = 16
HEAD_DIM = 128
D = 2048
TOK_DEV = 128
MB = 1
TOKENS = 4096
LAYERS = 8


def levels(rng, dims, pieces, least, largest):
    def one(dim, parts):
        draws = jax.random.uniform(jax.random.fold_in(jax.random.fold_in(rng, 6), dim), (parts,), jnp.float32, least / len(pieces), largest / len(pieces))
        return jnp.repeat(jnp.exp(draws), dims[dim] // parts).reshape((-1,) + (1,) * (len(dims) - dim - 1))

    gain = one(*pieces[0])
    for cut in pieces[1:]:
        gain = gain * one(*cut)
    return gain


def centred(own_key, shape, spread, most, split=(), kind=jnp.bfloat16):
    entries = spread * jax.random.normal(own_key, shape, jnp.float32)
    if split:
        entries = entries * levels(own_key, shape, split, -0.22, 0.18)
    return jnp.clip(entries, -most, most).astype(kind)


def setup_inputs(seed: int = 0) -> dict:
    streams_of = jax.random.split(jax.random.key(seed), 5)
    return {
        "tokens": centred(streams_of[0], (MB, TOKENS, D), 1.0, 6.0, ((1, 32),)),
        "w_qkv": centred(streams_of[1], (LAYERS, HEADS, HEAD_DIM, 3 * HEAD_DIM), HEAD_DIM ** -0.5, 0.5, ((0, 8),)),
        "norm_gain": jnp.clip(0.5 + 1.0 * jax.random.uniform(streams_of[2], (LAYERS, D), jnp.float32) ** levels(streams_of[2], (LAYERS, D), ((0, 8),), -0.2, 0.2), 0.5, 1.5),
        "out_gain": jnp.clip(0.5 + 1.0 * jax.random.uniform(streams_of[3], (LAYERS, D), jnp.float32) ** levels(streams_of[3], (LAYERS, D), ((0, 8),), -0.2, 0.2), 0.5, 1.5),
    }


epsilon = 1e-06

def rounded(value):
    return lax.optimization_barrier(value.astype(jnp.bfloat16)).astype(jnp.float32)

def one_layer(stream, gain_in, weights, gain_out):
    length = stream.shape[0]
    head_count = weights.shape[0]
    head_dim = weights.shape[1]
    widened = stream.astype(jnp.float32)
    normed = rounded(widened * lax.rsqrt(lax.optimization_barrier(jnp.mean(widened * widened, -1, keepdims=True)) + epsilon) * gain_in)
    projected = jnp.einsum('thd,hde->hte', normed.reshape(length, head_count, head_dim), weights.astype(jnp.float32))
    queries = rounded(projected[..., :head_dim] * head_dim ** (-0.5))
    keys_all = rounded(projected[..., head_dim:2 * head_dim])
    values_all = rounded(projected[..., 2 * head_dim:])
    blocks = length // TOK_DEV
    query_blocks = queries.reshape(head_count, blocks, TOK_DEV, head_dim)
    key_blocks = keys_all.reshape(head_count, blocks, TOK_DEV, head_dim)
    value_blocks = values_all.reshape(head_count, blocks, TOK_DEV, head_dim)
    kv_state = jnp.einsum('hbte,hbtf->hbef', key_blocks, value_blocks)
    running = jnp.cumsum(kv_state, axis=1)
    prefix = jnp.concatenate([jnp.zeros((head_count, 1, head_dim, head_dim), jnp.float32), running[:, :-1]], axis=1)
    prefix = rounded(prefix)
    scores = jnp.einsum('hbte,hbse->hbts', query_blocks, key_blocks)
    positions = jnp.arange(TOK_DEV, dtype=jnp.int32)
    causal = positions[:, None] >= positions[None, :]
    masked = rounded(jnp.where(causal, scores, 0.0))
    mixed_heads = jnp.einsum('hbts,hbsf->hbtf', masked, value_blocks) + jnp.einsum('hbte,hbef->hbtf', query_blocks, prefix)
    mixed_heads = mixed_heads * lax.rsqrt(lax.optimization_barrier(jnp.mean(mixed_heads * mixed_heads, -1, keepdims=True)) + epsilon)
    branch = jnp.transpose(mixed_heads.reshape(head_count, length, head_dim), (1, 0, 2)).reshape(length, head_count * head_dim)
    return (widened + branch * gain_out).astype(jnp.bfloat16)

def reference(tokens, w_qkv, norm_gain, out_gain):
    layer_outputs = []
    for layer_index in range(LAYERS):
        sequence_outputs = []
        for sequence_index in range(MB):
            stream = tokens[sequence_index] if layer_index == 0 else layer_outputs[-1][sequence_index]
            sequence_outputs.append(one_layer(stream, norm_gain[layer_index], w_qkv[layer_index], out_gain[layer_index]))
        layer_outputs.append(jnp.stack(sequence_outputs, 0))
    return jnp.stack(layer_outputs, 0)
```

```python
import functools

import jax
import jax.numpy as jnp
from jax import lax
from jax.experimental import pallas as pl
from jax.experimental.pallas import tpu as pltpu
from jax.sharding import Mesh, PartitionSpec as P

EPS = 1e-06
B = 128
ROWS = 144


def prepare_kernel(w_ref, gin_ref, gout_ref, out_ref):
    row = lax.broadcasted_iota(jnp.int32, (16, B), 0)
    for h in range(w_ref.shape[0]):
        out_ref[h, :B, :] = w_ref[h]
        rest = jnp.where(row == 0, gout_ref[h : h + 1, :], gin_ref[h : h + 1, :])
        for part in range(3):
            piece = rest.astype(jnp.bfloat16)
            out_ref[h, B:, part * B : (part + 1) * B] = piece
            rest = rest - piece.astype(jnp.float32)


def layer_kernel(chunks, info_ref, sums_ref, x_ref, w_ref, p_ref, xo_ref, po_ref, so_ref, r_ref, acc_ref):
    head = pl.program_id(0)
    heads = pl.num_programs(0)
    valid = info_ref[1] == 1

    @pl.when(head == 0)
    def _():
        r = lax.rsqrt(sums_ref[...] * (1.0 / 2048) + EPS)
        for c in range(chunks):
            r_ref[c * B : (c + 1) * B, :] = jnp.transpose(jnp.broadcast_to(r[c : c + 1, :], (B, B)))
        acc_ref[...] = jnp.zeros_like(acc_ref)

    @pl.when(jnp.logical_not(valid))
    def _():
        xo_ref[...] = x_ref[...]
        po_ref[...] = p_ref[...]
        for c in range(chunks):
            x = x_ref[c * B : (c + 1) * B, :].astype(jnp.float32)
            acc_ref[c * B : (c + 1) * B, :] += x * x

    @pl.when(valid)
    def _():
        causal = lax.broadcasted_iota(jnp.int32, (B, B), 0) >= lax.broadcasted_iota(jnp.int32, (B, B), 1)
        weights = w_ref[0, 0, :B, :]
        parts = w_ref[0, 0, B:, :].astype(jnp.float32)
        gains = parts[:, :B] + parts[:, B : 2 * B] + parts[:, 2 * B :]
        gain_out, gain_in = gains[:1], gains[1:2]
        prefix = p_ref[0].astype(jnp.float32)
        for c in range(chunks):
            rows = slice(c * B, (c + 1) * B)
            x = x_ref[rows, :].astype(jnp.float32)
            normed = (x * r_ref[rows, :] * gain_in).astype(jnp.bfloat16)
            qkv = jnp.dot(normed, weights, preferred_element_type=jnp.float32)
            q = (qkv[:, :B] * B**-0.5).astype(jnp.bfloat16)
            k = qkv[:, B : 2 * B].astype(jnp.bfloat16)
            v = qkv[:, 2 * B :].astype(jnp.bfloat16)
            scores = lax.dot_general(q, k, (((1,), (1,)), ((), ())), preferred_element_type=jnp.float32)
            scores = jnp.where(causal, scores, 0.0).astype(jnp.bfloat16)
            y = jnp.dot(
                jnp.concatenate([scores, q], 1),
                jnp.concatenate([v, prefix.astype(jnp.bfloat16)], 0),
                preferred_element_type=jnp.float32,
            )
            prefix = prefix + lax.dot_general(
                k, v, (((0,), (0,)), ((), ())), preferred_element_type=jnp.float32
            )
            mean = jnp.sum(y * y, 1, keepdims=True) * (1.0 / B)
            new = (x + y * lax.rsqrt(mean + EPS) * gain_out).astype(jnp.bfloat16)
            xo_ref[rows, :] = new
            new = new.astype(jnp.float32)
            acc_ref[rows, :] += new * new
        po_ref[0] = prefix.astype(jnp.bfloat16)

    @pl.when(head == heads - 1)
    def _():
        for c in range(chunks):
            so_ref[c : c + 1, :] = jnp.sum(jnp.transpose(acc_ref[c * B : (c + 1) * B, :]), 0, keepdims=True)


def layer(info, sums, x, weights, prefix):
    tokens, features = x.shape
    heads = features // B
    chunks = tokens // B
    spec = pltpu.PrefetchScalarGridSpec(
        num_scalar_prefetch=1,
        grid=(heads,),
        in_specs=[
            pl.BlockSpec((chunks, B), lambda h, info: (0, 0)),
            pl.BlockSpec((tokens, B), lambda h, info: (0, h)),
            pl.BlockSpec((1, 1, ROWS, 3 * B), lambda h, info: (info[0], h, 0, 0)),
            pl.BlockSpec((1, B, B), lambda h, info: (h, 0, 0)),
        ],
        out_specs=[
            pl.BlockSpec((tokens, B), lambda h, info: (0, h)),
            pl.BlockSpec((1, B, B), lambda h, info: (h, 0, 0)),
            pl.BlockSpec((chunks, B), lambda h, info: (0, 0)),
        ],
        scratch_shapes=[pltpu.VMEM((tokens, B), jnp.float32), pltpu.VMEM((tokens, B), jnp.float32)],
    )
    return pl.pallas_call(
        functools.partial(layer_kernel, chunks),
        grid_spec=spec,
        out_shape=[
            jax.ShapeDtypeStruct((tokens, features), jnp.bfloat16),
            jax.ShapeDtypeStruct((heads, B, B), jnp.bfloat16),
            jax.ShapeDtypeStruct((chunks, B), jnp.float32),
        ],
        compiler_params=pltpu.CompilerParams(
            dimension_semantics=("arbitrary",), vmem_limit_bytes=32 * 1024 * 1024
        ),
        cost_estimate=pl.CostEstimate(
            flops=tokens * features * 2 * 5 * B, bytes_accessed=4 * tokens * features, transcendentals=0
        ),
        name="layer",
    )(info, sums, x, weights, prefix)


def swap(block, axis):
    return lax.ppermute(block, axis, [(0, 1), (1, 0)])


def shards(tokens, w_qkv, norm_gain, out_gain):
    layers = lax.axis_size("z")
    segments = lax.axis_size("y")
    y, xh, xl, core, z = (lax.axis_index(a) for a in ("y", "xh", "xl", "core", "z"))
    groups = lax.axis_size("xl") * lax.axis_size("core")
    heads = w_qkv.shape[1] // groups
    features = heads * B
    group = xl * lax.axis_size("core") + core

    own_w = lax.dynamic_slice_in_dim(w_qkv[0], group * heads, heads, 0)
    own_in = lax.dynamic_slice_in_dim(norm_gain.reshape(-1, B), group * heads, heads, 0)
    own_out = lax.dynamic_slice_in_dim(out_gain.reshape(-1, B), group * heads, heads, 0)
    packed = pl.pallas_call(
        prepare_kernel,
        out_shape=jax.ShapeDtypeStruct((heads, ROWS, 3 * B), jnp.bfloat16),
        name="prepare",
    )(own_w, own_in, own_out)
    weights = lax.all_gather(packed, "z")

    block = tokens[0]
    count = block.shape[0]
    table = jnp.transpose(block.reshape(count, groups, features), (1, 0, 2))
    table = jnp.concatenate([table, table], 0)
    x = lax.all_to_all(table, ("xh", "xl", "core"), 0, 0, tiled=True)
    x = x.reshape(-1, features)
    wide = x.astype(jnp.float32)
    sums = jnp.sum(wide * wide, 1).reshape(-1, B)
    prefix = jnp.zeros((heads, B, B), jnp.bfloat16)

    ticks = layers + segments - 1
    for tick in range(ticks):
        sums = sums + swap(sums, "core")
        sums = sums + swap(sums, "xl")
        index = tick - y
        valid = (index >= 0) & (index <= z)
        info = jnp.stack([jnp.clip(index, 0, layers - 1), valid.astype(jnp.int32)])
        x, state, sums = layer(info, sums, x, weights, prefix)
        if tick + 1 < ticks:
            prefix = lax.ppermute(state, "y", [(i, i + 1) for i in range(segments - 1)])

    half = lax.dynamic_slice_in_dim(x, xh * (groups * count), groups * count, 0)
    out = lax.all_to_all(half.reshape(groups, count, features), ("xl", "core"), 0, 0, tiled=True)
    return jnp.transpose(out, (1, 0, 2)).reshape(1, 1, count, groups * features)


def solution(mesh):
    split = Mesh(mesh.devices.reshape(4, 2, 2, 2, 8), ("y", "xh", "xl", "core", "z"))
    ctx = ("y", "xh", "xl", "core")
    placed = (P(None, ctx, None), P("z", None, None, None), P("z", None), P("z", None))
    return jax.shard_map(
        shards, mesh=split, in_specs=placed, out_specs=P("z", None, ctx, None), check_vma=False
    )
```

```python
import jax
import jax.numpy as jnp
from jax import lax
from jax.experimental import pallas as pl
from jax.experimental.pallas import tpu as pltpu
from jax.sharding import Mesh, PartitionSpec as P

EPS = 1e-06
B = 128
ROWS = 144


def prepare_kernel(info_ref, w_ref, gin_ref, gout_ref, out_ref):
    row = lax.broadcasted_iota(jnp.int32, (16, B), 0)
    out_ref[0, :B, :] = w_ref[0]
    rest = jnp.where(row == 0, gout_ref[0], gin_ref[0])
    for part in range(3):
        piece = rest.astype(jnp.bfloat16)
        out_ref[0, B:, part * B : (part + 1) * B] = piece
        rest = rest - piece.astype(jnp.float32)


def prepare(group, heads, w_qkv, norm_gain, out_gain):
    def pick(h, info):
        return (info[0] * heads + h, 0, 0)

    return pl.pallas_call(
        prepare_kernel,
        grid_spec=pltpu.PrefetchScalarGridSpec(
            num_scalar_prefetch=1,
            grid=(heads,),
            in_specs=[pl.BlockSpec((1, B, 3 * B), pick), pl.BlockSpec((1, 1, B), pick), pl.BlockSpec((1, 1, B), pick)],
            out_specs=pl.BlockSpec((1, ROWS, 3 * B), lambda h, info: (h, 0, 0)),
        ),
        out_shape=jax.ShapeDtypeStruct((heads, ROWS, 3 * B), jnp.bfloat16),
        name="prepare",
    )(group.reshape(1), w_qkv, norm_gain.reshape(-1, 1, B), out_gain.reshape(-1, 1, B))


def mm(a, b, contract=(1, 0)):
    return lax.dot_general(a, b, (((contract[0],), (contract[1],)), ((), ())), preferred_element_type=jnp.float32)


def layer_kernel(
    info_ref, sums_ref, own_ref, x_ref, w_ref, p_ref,
    xo_ref, po_ref, so_ref, r_ref, acc_ref, q_ref, k_ref, v_ref, s_ref, kv_ref,
):
    tokens, features = x_ref.shape
    chunks = tokens // B
    valid = info_ref[0] == 1

    @pl.when(jnp.logical_not(valid))
    def _():
        po_ref[...] = p_ref[...]
        so_ref[...] = own_ref[...]

    @pl.when(valid)
    def _():
        r = lax.rsqrt(sums_ref[...] * (1.0 / 2048) + EPS)
        for c in range(chunks):
            r_ref[c * B : (c + 1) * B, :] = jnp.transpose(jnp.broadcast_to(r[c : c + 1, :], (B, B)))
        causal = lax.broadcasted_iota(jnp.int32, (B, B), 0) >= lax.broadcasted_iota(jnp.int32, (B, B), 1)
        for h in range(features // B):
            lanes = slice(h * B, (h + 1) * B)
            parts = w_ref[h, B:, :].astype(jnp.float32)
            gains = parts[:, :B] + parts[:, B : 2 * B] + parts[:, 2 * B :]
            gain_out, gain_in = gains[:1], gains[1:2]
            normed = (x_ref[:, lanes].astype(jnp.float32) * r_ref[...] * gain_in).astype(jnp.bfloat16)
            qkv = mm(normed, w_ref[h, :B, :])
            q_ref[...] = (qkv[:, :B] * B**-0.5).astype(jnp.bfloat16)
            k_ref[...] = qkv[:, B : 2 * B].astype(jnp.bfloat16)
            v_ref[...] = qkv[:, 2 * B :].astype(jnp.bfloat16)
            for c in range(chunks):
                rows = slice(c * B, (c + 1) * B)
                scores = mm(q_ref[rows, :], k_ref[rows, :], (1, 1))
                s_ref[rows, :] = jnp.where(causal, scores, 0.0).astype(jnp.bfloat16)
                kv_ref[c] = mm(k_ref[rows, :], v_ref[rows, :], (0, 0))
            prefix = p_ref[h].astype(jnp.float32)
            before = []
            for c in range(chunks):
                before.append(prefix.astype(jnp.bfloat16))
                prefix = prefix + kv_ref[c]
            po_ref[h] = prefix.astype(jnp.bfloat16)
            for c in range(chunks):
                rows = slice(c * B, (c + 1) * B)
                y = mm(
                    jnp.concatenate([s_ref[rows, :], q_ref[rows, :]], 1),
                    jnp.concatenate([v_ref[rows, :], before[c]], 0),
                )
                mean = jnp.sum(y * y, 1, keepdims=True) * (1.0 / B)
                new = (x_ref[rows, lanes].astype(jnp.float32) + y * lax.rsqrt(mean + EPS) * gain_out).astype(jnp.bfloat16)
                xo_ref[rows, lanes] = new
                new = new.astype(jnp.float32)
                square = new * new
                acc_ref[rows, :] = square if h == 0 else acc_ref[rows, :] + square
        for c in range(chunks):
            so_ref[c : c + 1, :] = jnp.sum(jnp.transpose(acc_ref[c * B : (c + 1) * B, :]), 0, keepdims=True)


def layer(valid, sums, own, x, weights, prefix):
    tokens, features = x.shape
    heads = features // B
    chunks = tokens // B
    whole = pl.BlockSpec(memory_space=pltpu.VMEM)
    half = pltpu.VMEM((tokens, B), jnp.bfloat16)
    full = pltpu.VMEM((tokens, B), jnp.float32)
    return pl.pallas_call(
        layer_kernel,
        in_specs=[pl.BlockSpec(memory_space=pltpu.SMEM)] + [whole] * 5,
        out_specs=[whole] * 3,
        out_shape=[
            jax.ShapeDtypeStruct((tokens, features), jnp.bfloat16),
            jax.ShapeDtypeStruct((heads, B, B), jnp.bfloat16),
            jax.ShapeDtypeStruct((chunks, B), jnp.float32),
        ],
        scratch_shapes=[full, full, half, half, half, half, pltpu.VMEM((chunks, B, B), jnp.float32)],
        input_output_aliases={3: 0},
        compiler_params=pltpu.CompilerParams(vmem_limit_bytes=16 * 1024 * 1024),
        cost_estimate=pl.CostEstimate(
            flops=tokens * features * 2 * 7 * B * 8, bytes_accessed=4 * tokens * features, transcendentals=0
        ),
        name="layer",
    )(valid.astype(jnp.int32).reshape(1), sums, own, x, weights, prefix)


def swap(block, axis):
    return lax.ppermute(block, axis, [(0, 1), (1, 0)])


def shards(tokens, w_qkv, norm_gain, out_gain):
    layers = lax.axis_size("z")
    segments = lax.axis_size("y")
    y, xh, xl, core, z = (lax.axis_index(a) for a in ("y", "xh", "xl", "core", "z"))
    groups = lax.axis_size("xl") * lax.axis_size("core")
    heads = w_qkv.shape[1] // groups
    features = heads * B
    group = xl * lax.axis_size("core") + core

    mine = prepare(group, heads, w_qkv[0], norm_gain, out_gain)
    rows = range(segments)

    def rotate(held, step):
        going = [row for row in rows if 0 <= step - row < layers]
        route = [(row * layers + a, row * layers + (a - 1) % layers) for row in going for a in range(layers)]
        return lax.ppermute(held, ("y", "z"), route)

    weights = rotate(mine, 0)

    block = tokens[0]
    count = block.shape[0]
    table = jnp.transpose(block.reshape(count, groups, features), (1, 0, 2))
    table = jnp.concatenate([table, table], 0)
    x = lax.all_to_all(table, ("xh", "xl", "core"), 0, 0, tiled=True)
    x = x.reshape(-1, features)
    wide = x.astype(jnp.float32)
    sums = jnp.sum(wide * wide, 1).reshape(-1, B)
    prefix = jnp.zeros((heads, B, B), jnp.bfloat16)

    own = sums
    ticks = layers + segments - 1
    for tick in range(ticks):
        step = tick - y + 1
        valid = (step >= layers - z) & (step <= layers)
        sums = own + swap(own, "core")
        sums = sums + swap(sums, "xl")
        if tick + 1 < ticks:
            held = jnp.where(y == tick + 1, mine, weights) if tick + 1 < segments else weights
            following = rotate(held, tick + 1)
        x, state, own = layer(valid, sums, own, x, weights, prefix)
        if tick + 1 < ticks:
            weights = following
            prefix = lax.ppermute(state, "y", [(i, i + 1) for i in range(segments - 1)])

    half = lax.dynamic_slice_in_dim(x, xh * (groups * count), groups * count, 0)
    out = lax.all_to_all(half.reshape(groups, count, features), ("xl", "core"), 0, 0, tiled=True)
    return jnp.transpose(out, (1, 0, 2)).reshape(1, 1, count, groups * features)


def solution(mesh):
    split = Mesh(mesh.devices.reshape(4, 2, 2, 2, 8), ("y", "xh", "xl", "core", "z"))
    ctx = ("y", "xh", "xl", "core")
    placed = (P(None, ctx, None), P("z", None, None, None), P("z", None), P("z", None))
    return jax.shard_map(
        shards, mesh=split, in_specs=placed, out_specs=P("z", None, ctx, None), check_vma=False
    )
```

```python
import jax
import jax.numpy as jnp
from jax import lax
from jax.experimental import pallas as pl
from jax.experimental.pallas import tpu as pltpu
from jax.sharding import Mesh, PartitionSpec as P

EPS = 1e-06
B = 128
GAINS = 16


def prepare_kernel(info_ref, w_ref, gin_ref, gout_ref, out_ref):
    heads = w_ref.shape[0]
    for h in range(heads):
        out_ref[h * B : (h + 1) * B, :] = w_ref[h]
    rest = jnp.concatenate([gout_ref[0], gin_ref[0], jnp.zeros((GAINS - 2 * heads, B), jnp.float32)], 0)
    for part in range(3):
        piece = rest.astype(jnp.bfloat16)
        out_ref[heads * B :, part * B : (part + 1) * B] = piece
        rest = rest - piece.astype(jnp.float32)


def prepare(group, groups, w_qkv, norm_gain, out_gain):
    heads = w_qkv.shape[0] // groups

    def pick(i, info):
        return (info[0], 0, 0)

    return pl.pallas_call(
        prepare_kernel,
        grid_spec=pltpu.PrefetchScalarGridSpec(
            num_scalar_prefetch=1,
            grid=(1,),
            in_specs=[
                pl.BlockSpec((heads, B, 3 * B), pick),
                pl.BlockSpec((1, heads, B), pick),
                pl.BlockSpec((1, heads, B), pick),
            ],
            out_specs=pl.BlockSpec((heads * B + GAINS, 3 * B), lambda i, info: (0, 0)),
        ),
        out_shape=jax.ShapeDtypeStruct((heads * B + GAINS, 3 * B), jnp.bfloat16),
        name="prepare",
    )(group.reshape(1), w_qkv, norm_gain.reshape(groups, heads, B), out_gain.reshape(groups, heads, B))


def spread_kernel(x_ref, out_ref):
    copies, _, width = out_ref.shape
    for i in range(copies):
        lane = i * width % x_ref.shape[1]
        out_ref[i] = x_ref[:, lane : lane + width]


def spread(block, copies, width):
    return pl.pallas_call(
        spread_kernel,
        out_shape=jax.ShapeDtypeStruct((copies, block.shape[0], width), block.dtype),
        name="spread",
    )(block)


def join_kernel(group_ref, *refs):
    parts, out_ref = refs[:-1], refs[-1]
    width = parts[0].shape[1]
    for j, part in enumerate(parts):
        lane = pl.multiple_of((group_ref[0] ^ j) * width, width)
        out_ref[:, pl.ds(lane, width)] = part[...]


def join(group, parts):
    rows, width = parts[0].shape
    whole = pl.BlockSpec(memory_space=pltpu.VMEM)
    return pl.pallas_call(
        join_kernel,
        in_specs=[pl.BlockSpec(memory_space=pltpu.SMEM)] + [whole] * len(parts),
        out_specs=whole,
        out_shape=jax.ShapeDtypeStruct((rows, width * len(parts)), jnp.bfloat16),
        name="join",
    )(group.reshape(1), *parts)


def mm(a, b, contract=(1, 0)):
    return lax.dot_general(a, b, (((contract[0],), (contract[1],)), ((), ())), preferred_element_type=jnp.float32)


def layer_kernel(
    info_ref, sums_ref, own_ref, x_ref, w_ref, p_ref,
    xo_ref, po_ref, so_ref, r_ref, acc_ref, q_ref, k_ref, v_ref, s_ref, kv_ref,
):
    tokens, features = x_ref.shape
    chunks = tokens // B
    valid = info_ref[0] == 1

    @pl.when(jnp.logical_not(valid))
    def _():
        po_ref[...] = p_ref[...]
        so_ref[...] = own_ref[...]

    @pl.when(valid)
    def _():
        r = lax.rsqrt(sums_ref[...] * (1.0 / 2048) + EPS)
        for c in range(chunks):
            r_ref[c * B : (c + 1) * B, :] = jnp.transpose(jnp.broadcast_to(r[c : c + 1, :], (B, B)))
        causal = lax.broadcasted_iota(jnp.int32, (B, B), 0) >= lax.broadcasted_iota(jnp.int32, (B, B), 1)
        heads = features // B
        parts = w_ref[heads * B :, :].astype(jnp.float32)
        gains = parts[:, :B] + parts[:, B : 2 * B] + parts[:, 2 * B :]
        for h in range(heads):
            lanes = slice(h * B, (h + 1) * B)
            gain_out, gain_in = gains[h : h + 1], gains[heads + h : heads + h + 1]
            normed = (x_ref[:, lanes].astype(jnp.float32) * r_ref[...] * gain_in).astype(jnp.bfloat16)
            qkv = mm(normed, w_ref[lanes, :])
            q_ref[...] = (qkv[:, :B] * B**-0.5).astype(jnp.bfloat16)
            k_ref[...] = qkv[:, B : 2 * B].astype(jnp.bfloat16)
            v_ref[...] = qkv[:, 2 * B :].astype(jnp.bfloat16)
            for c in range(chunks):
                rows = slice(c * B, (c + 1) * B)
                scores = mm(q_ref[rows, :], k_ref[rows, :], (1, 1))
                s_ref[rows, :] = jnp.where(causal, scores, 0.0).astype(jnp.bfloat16)
                kv_ref[c] = mm(k_ref[rows, :], v_ref[rows, :], (0, 0))
            prefix = p_ref[h].astype(jnp.float32)
            before = []
            for c in range(chunks):
                before.append(prefix.astype(jnp.bfloat16))
                prefix = prefix + kv_ref[c]
            po_ref[h] = prefix.astype(jnp.bfloat16)
            for c in range(chunks):
                rows = slice(c * B, (c + 1) * B)
                y = mm(
                    jnp.concatenate([s_ref[rows, :], q_ref[rows, :]], 1),
                    jnp.concatenate([v_ref[rows, :], before[c]], 0),
                )
                mean = jnp.sum(y * y, 1, keepdims=True) * (1.0 / B)
                new = (x_ref[rows, lanes].astype(jnp.float32) + y * lax.rsqrt(mean + EPS) * gain_out).astype(jnp.bfloat16)
                xo_ref[rows, lanes] = new
                new = new.astype(jnp.float32)
                square = new * new
                acc_ref[rows, :] = square if h == 0 else acc_ref[rows, :] + square
        for c in range(chunks):
            so_ref[c : c + 1, :] = jnp.sum(jnp.transpose(acc_ref[c * B : (c + 1) * B, :]), 0, keepdims=True)


def layer(valid, sums, own, x, weights, prefix):
    tokens, features = x.shape
    heads = features // B
    chunks = tokens // B
    whole = pl.BlockSpec(memory_space=pltpu.VMEM)
    half = pltpu.VMEM((tokens, B), jnp.bfloat16)
    full = pltpu.VMEM((tokens, B), jnp.float32)
    return pl.pallas_call(
        layer_kernel,
        in_specs=[pl.BlockSpec(memory_space=pltpu.SMEM)] + [whole] * 5,
        out_specs=[whole] * 3,
        out_shape=[
            jax.ShapeDtypeStruct((tokens, features), jnp.bfloat16),
            jax.ShapeDtypeStruct((heads, B, B), jnp.bfloat16),
            jax.ShapeDtypeStruct((chunks, B), jnp.float32),
        ],
        scratch_shapes=[full, full, half, half, half, half, pltpu.VMEM((chunks, B, B), jnp.float32)],
        input_output_aliases={3: 0},
        compiler_params=pltpu.CompilerParams(vmem_limit_bytes=16 * 1024 * 1024),
        cost_estimate=pl.CostEstimate(
            flops=tokens * features * 2 * 7 * B * 8, bytes_accessed=4 * tokens * features, transcendentals=0
        ),
        name="layer",
    )(valid.astype(jnp.int32).reshape(1), sums, own, x, weights, prefix)


def swap(block, axis):
    return lax.ppermute(block, axis, [(0, 1), (1, 0)])


def shards(tokens, w_qkv, norm_gain, out_gain):
    layers = lax.axis_size("z")
    segments = lax.axis_size("y")
    y, xh, xl, core, z = (lax.axis_index(a) for a in ("y", "xh", "xl", "core", "z"))
    groups = lax.axis_size("xl") * lax.axis_size("core")
    heads = w_qkv.shape[1] // groups
    features = heads * B
    group = xl * lax.axis_size("core") + core

    mine = prepare(group, groups, w_qkv[0], norm_gain, out_gain)
    rows = range(segments)

    def rotate(held, step):
        going = [row for row in rows if 0 <= step - row < layers]
        route = [(row * layers + a, row * layers + (a - 1) % layers) for row in going for a in range(layers)]
        return lax.ppermute(held, ("y", "z"), route)

    weights = rotate(mine, 0)

    block = tokens[0]
    count = block.shape[0]
    table = spread(block, 2 * groups, features)
    x = lax.all_to_all(table, ("xh", "xl", "core"), 0, 0, tiled=True)
    x = x.reshape(-1, features)
    wide = x.astype(jnp.float32)
    sums = jnp.sum(wide * wide, 1).reshape(-1, B)
    prefix = jnp.zeros((heads, B, B), jnp.bfloat16)

    own = sums
    ticks = layers + segments - 1
    for tick in range(ticks):
        step = tick - y + 1
        valid = (step >= layers - z) & (step <= layers)
        sums = own + swap(own, "core")
        sums = sums + swap(sums, "xl")
        if tick + 1 < ticks:
            held = jnp.where(y == tick + 1, mine, weights)
            following = rotate(held, tick + 1)
        x, state, own = layer(valid, sums, own, x, weights, prefix)
        if tick + 1 < ticks:
            weights = following
            prefix = lax.ppermute(state, "y", [(i, i + 1) for i in range(segments - 1)])

    def part(flip):
        place = ((xh * groups + group) ^ flip) * count
        rows = lax.dynamic_slice_in_dim(x, place, count, 0)
        route = [(i, i ^ flip) for i in range(2 * groups)]
        return lax.ppermute(rows, ("xh", "xl", "core"), route) if flip else rows

    return join(group, [part(0), part(1), part(2), part(7)]).reshape(1, 1, count, groups * features)


def solution(mesh):
    split = Mesh(mesh.devices.reshape(4, 2, 2, 2, 8), ("y", "xh", "xl", "core", "z"))
    ctx = ("y", "xh", "xl", "core")
    placed = (P(None, ctx, None), P("z", None, None, None), P("z", None), P("z", None))
    return jax.shard_map(
        shards, mesh=split, in_specs=placed, out_specs=P("z", None, ctx, None), check_vma=False
    )
```

```python
import jax
import jax.numpy as jnp
from jax import lax
from jax.experimental import pallas as pl
from jax.experimental.pallas import tpu as pltpu
from jax.sharding import Mesh, PartitionSpec as P

EPS = 1e-06
B = 128
GAINS = 16


def prepare_kernel(info_ref, w_ref, gin_ref, gout_ref, out_ref):
    heads = w_ref.shape[0]
    for h in range(heads):
        out_ref[h * B : (h + 1) * B, :] = w_ref[h]
    rest = jnp.concatenate([gout_ref[0], gin_ref[0], jnp.zeros((GAINS - 2 * heads, B), jnp.float32)], 0)
    for part in range(3):
        piece = rest.astype(jnp.bfloat16)
        out_ref[heads * B :, part * B : (part + 1) * B] = piece
        rest = rest - piece.astype(jnp.float32)


def prepare(group, groups, w_qkv, norm_gain, out_gain):
    heads = w_qkv.shape[0] // groups

    def pick(i, info):
        return (info[0], 0, 0)

    return pl.pallas_call(
        prepare_kernel,
        grid_spec=pltpu.PrefetchScalarGridSpec(
            num_scalar_prefetch=1,
            grid=(1,),
            in_specs=[
                pl.BlockSpec((heads, B, 3 * B), pick),
                pl.BlockSpec((1, heads, B), pick),
                pl.BlockSpec((1, heads, B), pick),
            ],
            out_specs=pl.BlockSpec((heads * B + GAINS, 3 * B), lambda i, info: (0, 0)),
        ),
        out_shape=jax.ShapeDtypeStruct((heads * B + GAINS, 3 * B), jnp.bfloat16),
        name="prepare",
    )(group.reshape(1), w_qkv, norm_gain.reshape(groups, heads, B), out_gain.reshape(groups, heads, B))


def spread_kernel(x_ref, out_ref):
    copies, _, width = out_ref.shape
    for i in range(copies):
        lane = i * width % x_ref.shape[1]
        out_ref[i] = x_ref[:, lane : lane + width]


def spread(block, copies, width):
    return pl.pallas_call(
        spread_kernel,
        out_shape=jax.ShapeDtypeStruct((copies, block.shape[0], width), block.dtype),
        name="spread",
    )(block)


def join_kernel(group_ref, *refs):
    parts, out_ref = refs[:-1], refs[-1]
    width = parts[0].shape[1]
    for j, part in enumerate(parts):
        lane = pl.multiple_of((group_ref[0] ^ j) * width, width)
        out_ref[:, pl.ds(lane, width)] = part[...]


def join(group, parts):
    rows, width = parts[0].shape
    whole = pl.BlockSpec(memory_space=pltpu.VMEM)
    return pl.pallas_call(
        join_kernel,
        in_specs=[pl.BlockSpec(memory_space=pltpu.SMEM)] + [whole] * len(parts),
        out_specs=whole,
        out_shape=jax.ShapeDtypeStruct((rows, width * len(parts)), jnp.bfloat16),
        name="join",
    )(group.reshape(1), *parts)


def mm(a, b, contract=(1, 0)):
    return lax.dot_general(a, b, (((contract[0],), (contract[1],)), ((), ())), preferred_element_type=jnp.float32)


def gains_of(w_ref, heads):
    parts = w_ref[heads * B :, :].astype(jnp.float32)
    return parts[:, :B] + parts[:, B : 2 * B] + parts[:, 2 * B :]


def project_kernel(info_ref, sums_ref, x_ref, w_ref, q_ref, v_ref, s_ref, before_ref, total_ref, r_ref, k_ref):
    tokens, features = x_ref.shape
    chunks = tokens // B
    heads = features // B

    @pl.when(info_ref[0] == 1)
    def _():
        r = lax.rsqrt(sums_ref[...] * (1.0 / 2048) + EPS)
        for c in range(chunks):
            r_ref[c * B : (c + 1) * B, :] = jnp.transpose(jnp.broadcast_to(r[c : c + 1, :], (B, B)))
        causal = lax.broadcasted_iota(jnp.int32, (B, B), 0) >= lax.broadcasted_iota(jnp.int32, (B, B), 1)
        gains = gains_of(w_ref, heads)
        for h in range(heads):
            lanes = slice(h * B, (h + 1) * B)
            gain_in = gains[heads + h : heads + h + 1]
            normed = (x_ref[:, lanes].astype(jnp.float32) * r_ref[...] * gain_in).astype(jnp.bfloat16)
            qkv = mm(normed, w_ref[lanes, :])
            q_ref[:, lanes] = (qkv[:, :B] * B**-0.5).astype(jnp.bfloat16)
            k_ref[...] = qkv[:, B : 2 * B].astype(jnp.bfloat16)
            v_ref[:, lanes] = qkv[:, 2 * B :].astype(jnp.bfloat16)
            total = jnp.zeros((B, B), jnp.float32)
            for c in range(chunks):
                rows = slice(c * B, (c + 1) * B)
                scores = mm(q_ref[rows, lanes], k_ref[rows, :], (1, 1))
                s_ref[rows, lanes] = jnp.where(causal, scores, 0.0).astype(jnp.bfloat16)
                before_ref[h, c] = total
                total = total + mm(k_ref[rows, :], v_ref[rows, lanes], (0, 0))
            total_ref[h] = total


def mix_kernel(info_ref, own_ref, x_ref, w_ref, q_ref, v_ref, s_ref, before_ref, p_ref, xo_ref, so_ref):
    tokens, features = x_ref.shape
    chunks = tokens // B
    heads = features // B
    valid = info_ref[0] == 1

    @pl.when(jnp.logical_not(valid))
    def _():
        so_ref[...] = own_ref[...]

    @pl.when(valid)
    def _():
        gains = gains_of(w_ref, heads)
        for c in range(chunks):
            rows = slice(c * B, (c + 1) * B)
            squares = None
            for h in range(heads):
                lanes = slice(h * B, (h + 1) * B)
                prefix = (p_ref[h].astype(jnp.float32) + before_ref[h, c]).astype(jnp.bfloat16)
                y = mm(
                    jnp.concatenate([s_ref[rows, lanes], q_ref[rows, lanes]], 1),
                    jnp.concatenate([v_ref[rows, lanes], prefix], 0),
                )
                mean = jnp.sum(y * y, 1, keepdims=True) * (1.0 / B)
                old = x_ref[rows, lanes].astype(jnp.float32)
                new = (old + y * lax.rsqrt(mean + EPS) * gains[h : h + 1]).astype(jnp.bfloat16)
                xo_ref[rows, lanes] = new
                new = new.astype(jnp.float32)
                squares = new * new if squares is None else squares + new * new
            so_ref[c : c + 1, :] = jnp.sum(jnp.transpose(squares), 0, keepdims=True)


def project(valid, sums, x, weights):
    tokens, features = x.shape
    heads = features // B
    chunks = tokens // B
    whole = pl.BlockSpec(memory_space=pltpu.VMEM)
    wide = jax.ShapeDtypeStruct((tokens, features), jnp.bfloat16)
    return pl.pallas_call(
        project_kernel,
        in_specs=[pl.BlockSpec(memory_space=pltpu.SMEM)] + [whole] * 3,
        out_specs=[whole] * 5,
        out_shape=[
            wide, wide, wide,
            jax.ShapeDtypeStruct((heads, chunks, B, B), jnp.float32),
            jax.ShapeDtypeStruct((heads, B, B), jnp.float32),
        ],
        scratch_shapes=[pltpu.VMEM((tokens, B), jnp.float32), pltpu.VMEM((tokens, B), jnp.bfloat16)],
        compiler_params=pltpu.CompilerParams(vmem_limit_bytes=8 * 1024 * 1024),
        cost_estimate=pl.CostEstimate(
            flops=tokens * features * 2 * 5 * B * 4, bytes_accessed=tokens * features, transcendentals=0
        ),
        name="project",
    )(valid, sums, x, weights)


def mix(valid, own, x, weights, q, v, s, before, prefix):
    tokens, features = x.shape
    whole = pl.BlockSpec(memory_space=pltpu.VMEM)
    return pl.pallas_call(
        mix_kernel,
        in_specs=[pl.BlockSpec(memory_space=pltpu.SMEM)] + [whole] * 8,
        out_specs=[whole] * 2,
        out_shape=[
            jax.ShapeDtypeStruct((tokens, features), jnp.bfloat16),
            jax.ShapeDtypeStruct((tokens // B, B), jnp.float32),
        ],
        input_output_aliases={2: 0},
        compiler_params=pltpu.CompilerParams(vmem_limit_bytes=8 * 1024 * 1024),
        cost_estimate=pl.CostEstimate(
            flops=tokens * features * 2 * 4 * B * 4, bytes_accessed=tokens * features, transcendentals=0
        ),
        name="mix",
    )(valid, own, x, weights, q, v, s, before, prefix)


def swap(block, axis):
    return lax.ppermute(block, axis, [(0, 1), (1, 0)])


def shards(tokens, w_qkv, norm_gain, out_gain):
    layers = lax.axis_size("z")
    segments = lax.axis_size("y")
    y, xh, xl, core, z = (lax.axis_index(a) for a in ("y", "xh", "xl", "core", "z"))
    groups = lax.axis_size("xl") * lax.axis_size("core")
    heads = w_qkv.shape[1] // groups
    features = heads * B
    group = xl * lax.axis_size("core") + core

    mine = prepare(group, groups, w_qkv[0], norm_gain, out_gain)
    rows = range(segments)

    def rotate(held, step):
        going = [row for row in rows if 0 <= step - row < layers]
        route = [(row * layers + a, row * layers + (a - 1) % layers) for row in going for a in range(layers)]
        return lax.ppermute(held, ("y", "z"), route)

    weights = rotate(mine, 0)

    block = tokens[0]
    count = block.shape[0]
    table = spread(block, 2 * groups, features)
    x = lax.all_to_all(table, ("xh", "xl", "core"), 0, 0, tiled=True)
    x = x.reshape(-1, features)
    wide = x.astype(jnp.float32)
    sums = jnp.sum(wide * wide, 1).reshape(-1, B)
    arriving = jnp.zeros((heads, B, B), jnp.bfloat16)

    own = sums
    ticks = layers + segments - 1
    for tick in range(ticks):
        step = tick - y + 1
        valid = ((step >= layers - z) & (step <= layers)).astype(jnp.int32).reshape(1)
        sums = own + swap(own, "core")
        sums = sums + swap(sums, "xl")
        if tick + 1 < ticks:
            held = jnp.where(y == tick + 1, mine, weights)
            following = rotate(held, tick + 1)
        q, v, s, before, total = project(valid, sums, x, weights)
        prefix = arriving
        if tick + 1 < ticks:
            state = (prefix.astype(jnp.float32) + total).astype(jnp.bfloat16)
            arriving = lax.ppermute(state, "y", [(i, i + 1) for i in range(segments - 1)])
        x, own = mix(valid, own, x, weights, q, v, s, before, prefix)
        if tick + 1 < ticks:
            weights = following

    def part(flip):
        place = ((xh * groups + group) ^ flip) * count
        rows = lax.dynamic_slice_in_dim(x, place, count, 0)
        route = [(i, i ^ flip) for i in range(2 * groups)]
        return lax.ppermute(rows, ("xh", "xl", "core"), route) if flip else rows

    return join(group, [part(0), part(1), part(2), part(7)]).reshape(1, 1, count, groups * features)


def solution(mesh):
    split = Mesh(mesh.devices.reshape(4, 2, 2, 2, 8), ("y", "xh", "xl", "core", "z"))
    ctx = ("y", "xh", "xl", "core")
    placed = (P(None, ctx, None), P("z", None, None, None), P("z", None), P("z", None))
    return jax.shard_map(
        shards, mesh=split, in_specs=placed, out_specs=P("z", None, ctx, None), check_vma=False
    )
```

```python
import jax
import jax.numpy as jnp
from jax import lax
from jax.experimental import pallas as pl
from jax.experimental.pallas import tpu as pltpu
from jax.sharding import Mesh, PartitionSpec as P

EPS = 1e-06
B = 128
GAINS = 16


def prepare_kernel(info_ref, w_ref, gin_ref, gout_ref, out_ref):
    heads = w_ref.shape[0]
    for h in range(heads):
        out_ref[h * B : (h + 1) * B, :] = w_ref[h]
    rest = jnp.concatenate([gout_ref[0], gin_ref[0], jnp.zeros((GAINS - 2 * heads, B), jnp.float32)], 0)
    for part in range(3):
        piece = rest.astype(jnp.bfloat16)
        out_ref[heads * B :, part * B : (part + 1) * B] = piece
        rest = rest - piece.astype(jnp.float32)


def prepare(group, groups, w_qkv, norm_gain, out_gain):
    heads = w_qkv.shape[0] // groups

    def pick(i, info):
        return (info[0], 0, 0)

    return pl.pallas_call(
        prepare_kernel,
        grid_spec=pltpu.PrefetchScalarGridSpec(
            num_scalar_prefetch=1,
            grid=(1,),
            in_specs=[
                pl.BlockSpec((heads, B, 3 * B), pick),
                pl.BlockSpec((1, heads, B), pick),
                pl.BlockSpec((1, heads, B), pick),
            ],
            out_specs=pl.BlockSpec((heads * B + GAINS, 3 * B), lambda i, info: (0, 0)),
        ),
        out_shape=jax.ShapeDtypeStruct((heads * B + GAINS, 3 * B), jnp.bfloat16),
        name="prepare",
    )(group.reshape(1), w_qkv, norm_gain.reshape(groups, heads, B), out_gain.reshape(groups, heads, B))


def spread_kernel(x_ref, out_ref):
    copies, _, width = out_ref.shape
    for i in range(copies):
        lane = i * width % x_ref.shape[1]
        out_ref[i] = x_ref[:, lane : lane + width]


def spread(block, copies, width):
    return pl.pallas_call(
        spread_kernel,
        out_shape=jax.ShapeDtypeStruct((copies, block.shape[0], width), block.dtype),
        name="spread",
    )(block)


def join_kernel(group_ref, *refs):
    parts, out_ref = refs[:-1], refs[-1]
    width = parts[0].shape[1]
    for j, part in enumerate(parts):
        lane = pl.multiple_of((group_ref[0] ^ j) * width, width)
        out_ref[:, pl.ds(lane, width)] = part[...]


def join(group, parts):
    rows, width = parts[0].shape
    whole = pl.BlockSpec(memory_space=pltpu.VMEM)
    return pl.pallas_call(
        join_kernel,
        in_specs=[pl.BlockSpec(memory_space=pltpu.SMEM)] + [whole] * len(parts),
        out_specs=whole,
        out_shape=jax.ShapeDtypeStruct((rows, width * len(parts)), jnp.bfloat16),
        name="join",
    )(group.reshape(1), *parts)


def mm(a, b, contract=(1, 0)):
    return lax.dot_general(a, b, (((contract[0],), (contract[1],)), ((), ())), preferred_element_type=jnp.float32)


def gains_of(w_ref, heads):
    parts = w_ref[heads * B :, :].astype(jnp.float32)
    return parts[:, :B] + parts[:, B : 2 * B] + parts[:, 2 * B :]


def project_kernel(info_ref, sums_ref, x_ref, w_ref, q_ref, v_ref, s_ref, before_ref, total_ref, r_ref, k_ref):
    tokens, features = x_ref.shape
    chunks = tokens // B
    heads = features // B

    @pl.when(info_ref[0] == 1)
    def _():
        r = lax.rsqrt(sums_ref[...] * (1.0 / 2048) + EPS)
        for c in range(chunks):
            r_ref[c * B : (c + 1) * B, :] = jnp.transpose(jnp.broadcast_to(r[c : c + 1, :], (B, B)))
        causal = lax.broadcasted_iota(jnp.int32, (B, B), 0) >= lax.broadcasted_iota(jnp.int32, (B, B), 1)
        gains = gains_of(w_ref, heads)
        for h in range(heads):
            lanes = slice(h * B, (h + 1) * B)
            gain_in = gains[heads + h : heads + h + 1]
            normed = (x_ref[:, lanes].astype(jnp.float32) * r_ref[...] * gain_in).astype(jnp.bfloat16)
            qkv = mm(normed, w_ref[lanes, :])
            q_ref[:, lanes] = (qkv[:, :B] * B**-0.5).astype(jnp.bfloat16)
            k_ref[...] = qkv[:, B : 2 * B].astype(jnp.bfloat16)
            v_ref[:, lanes] = qkv[:, 2 * B :].astype(jnp.bfloat16)
            total = jnp.zeros((B, B), jnp.float32)
            for c in range(chunks):
                rows = slice(c * B, (c + 1) * B)
                scores = mm(q_ref[rows, lanes], k_ref[rows, :], (1, 1))
                s_ref[rows, lanes] = jnp.where(causal, scores, 0.0).astype(jnp.bfloat16)
                before_ref[h, c] = total
                total = total + mm(k_ref[rows, :], v_ref[rows, lanes], (0, 0))
            total_ref[h] = total


def mix_kernel(info_ref, own_ref, x_ref, w_ref, q_ref, v_ref, s_ref, before_ref, p_ref, xo_ref, so_ref):
    tokens, features = x_ref.shape
    chunks = tokens // B
    heads = features // B
    valid = info_ref[0] == 1

    @pl.when(jnp.logical_not(valid))
    def _():
        so_ref[...] = own_ref[...]

    @pl.when(valid)
    def _():
        gains = gains_of(w_ref, heads)
        for c in range(chunks):
            rows = slice(c * B, (c + 1) * B)
            squares = None
            for h in range(heads):
                lanes = slice(h * B, (h + 1) * B)
                prefix = (p_ref[h].astype(jnp.float32) + before_ref[h, c]).astype(jnp.bfloat16)
                y = mm(
                    jnp.concatenate([s_ref[rows, lanes], q_ref[rows, lanes]], 1),
                    jnp.concatenate([v_ref[rows, lanes], prefix], 0),
                )
                mean = jnp.sum(y * y, 1, keepdims=True) * (1.0 / B)
                old = x_ref[rows, lanes].astype(jnp.float32)
                new = (old + y * lax.rsqrt(mean + EPS) * gains[h : h + 1]).astype(jnp.bfloat16)
                xo_ref[rows, lanes] = new
                new = new.astype(jnp.float32)
                squares = new * new if squares is None else squares + new * new
            so_ref[c : c + 1, :] = jnp.sum(jnp.transpose(squares), 0, keepdims=True)


def project(valid, sums, x, weights):
    tokens, features = x.shape
    heads = features // B
    chunks = tokens // B
    whole = pl.BlockSpec(memory_space=pltpu.VMEM)
    wide = jax.ShapeDtypeStruct((tokens, features), jnp.bfloat16)
    return pl.pallas_call(
        project_kernel,
        in_specs=[pl.BlockSpec(memory_space=pltpu.SMEM)] + [whole] * 3,
        out_specs=[whole] * 5,
        out_shape=[
            wide, wide, wide,
            jax.ShapeDtypeStruct((heads, chunks, B, B), jnp.float32),
            jax.ShapeDtypeStruct((heads, B, B), jnp.float32),
        ],
        scratch_shapes=[pltpu.VMEM((tokens, B), jnp.float32), pltpu.VMEM((tokens, B), jnp.bfloat16)],
        compiler_params=pltpu.CompilerParams(vmem_limit_bytes=8 * 1024 * 1024),
        cost_estimate=pl.CostEstimate(
            flops=tokens * features * 2 * 5 * B * 4, bytes_accessed=tokens * features, transcendentals=0
        ),
        name="project",
    )(valid, sums, x, weights)


def mix(valid, own, x, weights, q, v, s, before, prefix):
    tokens, features = x.shape
    whole = pl.BlockSpec(memory_space=pltpu.VMEM)
    return pl.pallas_call(
        mix_kernel,
        in_specs=[pl.BlockSpec(memory_space=pltpu.SMEM)] + [whole] * 8,
        out_specs=[whole] * 2,
        out_shape=[
            jax.ShapeDtypeStruct((tokens, features), jnp.bfloat16),
            jax.ShapeDtypeStruct((tokens // B, B), jnp.float32),
        ],
        input_output_aliases={2: 0},
        compiler_params=pltpu.CompilerParams(vmem_limit_bytes=8 * 1024 * 1024),
        cost_estimate=pl.CostEstimate(
            flops=tokens * features * 2 * 4 * B * 4, bytes_accessed=tokens * features, transcendentals=0
        ),
        name="mix",
    )(valid, own, x, weights, q, v, s, before, prefix)


def swap(block, axis):
    return lax.ppermute(block, axis, [(0, 1), (1, 0)])


def shards(tokens, w_qkv, norm_gain, out_gain):
    layers = lax.axis_size("z")
    segments = lax.axis_size("y")
    y, xh, xl, core, z = (lax.axis_index(a) for a in ("y", "xh", "xl", "core", "z"))
    groups = lax.axis_size("xl") * lax.axis_size("core")
    heads = w_qkv.shape[1] // groups
    features = heads * B
    group = xl * lax.axis_size("core") + core

    mine = prepare(group, groups, w_qkv[0], norm_gain, out_gain)
    rows = range(segments)

    def rotate(held, step):
        going = [row for row in rows if 0 <= step - row < layers]
        route = [(row * layers + a, row * layers + (a - 1) % layers) for row in going for a in range(layers)]
        return lax.ppermute(held, ("y", "z"), route)

    weights = rotate(mine, 0)
    every = lax.all_gather(mine, "z")

    block = tokens[0]
    count = block.shape[0]
    table = spread(block, 2 * groups, features)
    x = lax.all_to_all(table, ("xh", "xl", "core"), 0, 0, tiled=True)
    x = x.reshape(-1, features)
    wide = x.astype(jnp.float32)
    sums = jnp.sum(wide * wide, 1).reshape(-1, B)
    arriving = jnp.zeros((heads, B, B), jnp.bfloat16)

    own = sums
    ticks = layers + segments - 1
    for tick in range(ticks):
        step = tick - y + 1
        valid = ((step >= layers - z) & (step <= layers)).astype(jnp.int32).reshape(1)
        sums = own + swap(own, "core")
        sums = sums + swap(sums, "xl")
        if tick + 1 < segments:
            held = jnp.where(y == tick + 1, mine, weights)
            following = rotate(held, tick + 1)
        elif tick + 1 < ticks:
            index = jnp.clip(z + step + 1 - layers, 0, layers - 1)
            following = lax.dynamic_index_in_dim(every, index, 0, keepdims=False)
        q, v, s, before, total = project(valid, sums, x, weights)
        prefix = arriving
        if tick + 1 < ticks:
            state = (prefix.astype(jnp.float32) + total).astype(jnp.bfloat16)
            arriving = lax.ppermute(state, "y", [(i, i + 1) for i in range(segments - 1)])
        x, own = mix(valid, own, x, weights, q, v, s, before, prefix)
        if tick + 1 < ticks:
            weights = following

    def part(flip):
        place = ((xh * groups + group) ^ flip) * count
        rows = lax.dynamic_slice_in_dim(x, place, count, 0)
        route = [(i, i ^ flip) for i in range(2 * groups)]
        return lax.ppermute(rows, ("xh", "xl", "core"), route) if flip else rows

    return join(group, [part(0), part(1), part(2), part(7)]).reshape(1, 1, count, groups * features)


def solution(mesh):
    split = Mesh(mesh.devices.reshape(4, 2, 2, 2, 8), ("y", "xh", "xl", "core", "z"))
    ctx = ("y", "xh", "xl", "core")
    placed = (P(None, ctx, None), P("z", None, None, None), P("z", None), P("z", None))
    return jax.shard_map(
        shards, mesh=split, in_specs=placed, out_specs=P("z", None, ctx, None), check_vma=False
    )
```

```python
import jax
import jax.numpy as jnp
from jax import lax
from jax.experimental import pallas as pl
from jax.experimental.pallas import tpu as pltpu
from jax.sharding import Mesh, PartitionSpec as P

EPS = 1e-06
B = 128
GAINS = 16


def prepare_kernel(info_ref, w_ref, gin_ref, gout_ref, out_ref):
    heads = w_ref.shape[0]
    for h in range(heads):
        out_ref[h * B : (h + 1) * B, :] = w_ref[h]
    rest = jnp.concatenate([gout_ref[0], gin_ref[0], jnp.zeros((GAINS - 2 * heads, B), jnp.float32)], 0)
    for part in range(3):
        piece = rest.astype(jnp.bfloat16)
        out_ref[heads * B :, part * B : (part + 1) * B] = piece
        rest = rest - piece.astype(jnp.float32)


def prepare(group, groups, w_qkv, norm_gain, out_gain):
    heads = w_qkv.shape[0] // groups

    def pick(i, info):
        return (info[0], 0, 0)

    return pl.pallas_call(
        prepare_kernel,
        grid_spec=pltpu.PrefetchScalarGridSpec(
            num_scalar_prefetch=1,
            grid=(1,),
            in_specs=[
                pl.BlockSpec((heads, B, 3 * B), pick),
                pl.BlockSpec((1, heads, B), pick),
                pl.BlockSpec((1, heads, B), pick),
            ],
            out_specs=pl.BlockSpec((heads * B + GAINS, 3 * B), lambda i, info: (0, 0)),
        ),
        out_shape=jax.ShapeDtypeStruct((heads * B + GAINS, 3 * B), jnp.bfloat16),
        name="prepare",
    )(group.reshape(1), w_qkv, norm_gain.reshape(groups, heads, B), out_gain.reshape(groups, heads, B))


def spread_kernel(x_ref, out_ref, sums_ref):
    x = x_ref[...]
    for i in range(out_ref.shape[0]):
        out_ref[i, 0] = x
    x = x.astype(jnp.float32)
    sums = jnp.sum(jnp.transpose(x * x), 0, keepdims=True)

    @pl.when(pl.program_id(0) == 0)
    def _():
        sums_ref[...] = sums

    @pl.when(pl.program_id(0) > 0)
    def _():
        sums_ref[...] += sums


def spread(block, copies, width):
    count, total = block.shape
    groups = total // width
    table, sums = pl.pallas_call(
        spread_kernel,
        grid=(groups,),
        in_specs=[pl.BlockSpec((count, width), lambda g: (0, g))],
        out_specs=[
            pl.BlockSpec((copies, 1, count, width), lambda g: (0, g, 0, 0)),
            pl.BlockSpec((1, count), lambda g: (0, 0)),
        ],
        out_shape=[
            jax.ShapeDtypeStruct((copies, groups, count, width), block.dtype),
            jax.ShapeDtypeStruct((1, count), jnp.float32),
        ],
        name="spread",
    )(block)
    return table.reshape(copies * groups, count, width), sums


def join_kernel(group_ref, *refs):
    parts, out_ref = refs[:-1], refs[-1]
    width = parts[0].shape[1]
    for j, part in enumerate(parts):
        lane = pl.multiple_of((group_ref[0] ^ j) * width, width)
        out_ref[:, pl.ds(lane, width)] = part[...]


def join(group, parts):
    rows, width = parts[0].shape
    whole = pl.BlockSpec(memory_space=pltpu.VMEM)
    return pl.pallas_call(
        join_kernel,
        in_specs=[pl.BlockSpec(memory_space=pltpu.SMEM)] + [whole] * len(parts),
        out_specs=whole,
        out_shape=jax.ShapeDtypeStruct((rows, width * len(parts)), jnp.bfloat16),
        name="join",
    )(group.reshape(1), *parts)


def mm(a, b, contract=(1, 0)):
    return lax.dot_general(a, b, (((contract[0],), (contract[1],)), ((), ())), preferred_element_type=jnp.float32)


def gains_of(w_ref, heads):
    parts = w_ref[heads * B :, :].astype(jnp.float32)
    return parts[:, :B] + parts[:, B : 2 * B] + parts[:, 2 * B :]


def project_kernel(info_ref, sums_ref, x_ref, w_ref, q_ref, v_ref, s_ref, before_ref, total_ref, r_ref, k_ref):
    tokens, features = x_ref.shape
    chunks = tokens // B
    heads = features // B

    @pl.when(info_ref[0] == 1)
    def _():
        r = lax.rsqrt(sums_ref[...] * (1.0 / 2048) + EPS)
        for c in range(chunks):
            r_ref[c * B : (c + 1) * B, :] = jnp.transpose(jnp.broadcast_to(r[c : c + 1, :], (B, B)))
        causal = lax.broadcasted_iota(jnp.int32, (B, B), 0) >= lax.broadcasted_iota(jnp.int32, (B, B), 1)
        gains = gains_of(w_ref, heads)
        for h in range(heads):
            lanes = slice(h * B, (h + 1) * B)
            gain_in = gains[heads + h : heads + h + 1]
            normed = (x_ref[:, lanes].astype(jnp.float32) * r_ref[...] * gain_in).astype(jnp.bfloat16)
            qkv = mm(normed, w_ref[lanes, :])
            q_ref[:, lanes] = (qkv[:, :B] * B**-0.5).astype(jnp.bfloat16)
            k_ref[...] = qkv[:, B : 2 * B].astype(jnp.bfloat16)
            v_ref[:, lanes] = qkv[:, 2 * B :].astype(jnp.bfloat16)
            total = jnp.zeros((B, B), jnp.float32)
            for c in range(chunks):
                rows = slice(c * B, (c + 1) * B)
                scores = mm(q_ref[rows, lanes], k_ref[rows, :], (1, 1))
                s_ref[rows, lanes] = jnp.where(causal, scores, 0.0).astype(jnp.bfloat16)
                before_ref[h, c] = total
                total = total + mm(k_ref[rows, :], v_ref[rows, lanes], (0, 0))
            total_ref[h] = total


def mix_kernel(info_ref, own_ref, x_ref, w_ref, next_ref, q_ref, v_ref, s_ref, before_ref, p_ref, xo_ref, so_ref):
    tokens, features = x_ref.shape
    chunks = tokens // B
    heads = features // B
    valid = info_ref[0] == 1

    @pl.when(jnp.logical_not(valid))
    def _():
        so_ref[...] = own_ref[...]

    @pl.when(valid)
    def _():
        gains = gains_of(w_ref, heads)
        for c in range(chunks):
            rows = slice(c * B, (c + 1) * B)
            squares = None
            for h in range(heads):
                lanes = slice(h * B, (h + 1) * B)
                prefix = (p_ref[h].astype(jnp.float32) + before_ref[h, c]).astype(jnp.bfloat16)
                y = mm(
                    jnp.concatenate([s_ref[rows, lanes], q_ref[rows, lanes]], 1),
                    jnp.concatenate([v_ref[rows, lanes], prefix], 0),
                )
                mean = jnp.sum(y * y, 1, keepdims=True) * (1.0 / B)
                old = x_ref[rows, lanes].astype(jnp.float32)
                new = (old + y * lax.rsqrt(mean + EPS) * gains[h : h + 1]).astype(jnp.bfloat16)
                xo_ref[rows, lanes] = new
                new = new.astype(jnp.float32)
                squares = new * new if squares is None else squares + new * new
            so_ref[c : c + 1, :] = jnp.sum(jnp.transpose(squares), 0, keepdims=True)


def project(valid, sums, x, weights):
    tokens, features = x.shape
    heads = features // B
    chunks = tokens // B
    whole = pl.BlockSpec(memory_space=pltpu.VMEM)
    wide = jax.ShapeDtypeStruct((tokens, features), jnp.bfloat16)
    return pl.pallas_call(
        project_kernel,
        in_specs=[pl.BlockSpec(memory_space=pltpu.SMEM)] + [whole] * 3,
        out_specs=[whole] * 5,
        out_shape=[
            wide, wide, wide,
            jax.ShapeDtypeStruct((heads, chunks, B, B), jnp.float32),
            jax.ShapeDtypeStruct((heads, B, B), jnp.float32),
        ],
        scratch_shapes=[pltpu.VMEM((tokens, B), jnp.float32), pltpu.VMEM((tokens, B), jnp.bfloat16)],
        compiler_params=pltpu.CompilerParams(vmem_limit_bytes=8 * 1024 * 1024),
        cost_estimate=pl.CostEstimate(
            flops=tokens * features * 2 * 5 * B * 4, bytes_accessed=tokens * features, transcendentals=0
        ),
        name="project",
    )(valid, sums, x, weights)


def mix(valid, own, x, weights, following, q, v, s, before, prefix):
    tokens, features = x.shape
    whole = pl.BlockSpec(memory_space=pltpu.VMEM)
    return pl.pallas_call(
        mix_kernel,
        in_specs=[pl.BlockSpec(memory_space=pltpu.SMEM)] + [whole] * 3 + [pl.BlockSpec(memory_space=pl.ANY)] + [whole] * 5,
        out_specs=[whole] * 2,
        out_shape=[
            jax.ShapeDtypeStruct((tokens, features), jnp.bfloat16),
            jax.ShapeDtypeStruct((tokens // B, B), jnp.float32),
        ],
        input_output_aliases={2: 0},
        compiler_params=pltpu.CompilerParams(vmem_limit_bytes=8 * 1024 * 1024),
        cost_estimate=pl.CostEstimate(
            flops=tokens * features * 2 * 4 * B * 4, bytes_accessed=tokens * features, transcendentals=0
        ),
        name="mix",
    )(valid, own, x, weights, following, q, v, s, before, prefix)


def swap(block, axis):
    return lax.ppermute(block, axis, [(0, 1), (1, 0)])


def shards(tokens, w_qkv, norm_gain, out_gain):
    layers = lax.axis_size("z")
    segments = lax.axis_size("y")
    y, xh, xl, core, z = (lax.axis_index(a) for a in ("y", "xh", "xl", "core", "z"))
    groups = lax.axis_size("xl") * lax.axis_size("core")
    heads = w_qkv.shape[1] // groups
    features = heads * B
    group = xl * lax.axis_size("core") + core

    mine = prepare(group, groups, w_qkv[0], norm_gain, out_gain)
    rows = range(segments)

    def rotate(held, step):
        going = [row for row in rows if 0 <= step - row < layers]
        route = [(row * layers + a, row * layers + (a - 1) % layers) for row in going for a in range(layers)]
        return lax.ppermute(held, ("y", "z"), route)

    weights = rotate(mine, 0)

    block = tokens[0]
    count = block.shape[0]
    table, total = spread(block, 2, features)
    x = lax.all_to_all(table, ("xh", "xl", "core"), 0, 0, tiled=True)
    x = x.reshape(-1, features)
    for axis, place in (("core", core), ("xl", xl), ("xh", xh)):
        other = swap(total, axis)
        low, high = jnp.where(place == 0, total, other), jnp.where(place == 0, other, total)
        total = jnp.concatenate([low, high], 0)
    own = total * (1.0 / groups)
    arriving = jnp.zeros((heads, B, B), jnp.bfloat16)

    ticks = layers + segments - 1
    for tick in range(ticks):
        step = tick - y + 1
        valid = ((step >= layers - z) & (step <= layers)).astype(jnp.int32).reshape(1)
        sums = total
        if tick:
            sums = own + swap(own, "core")
            sums = sums + swap(sums, "xl")
        following = rotate(jnp.where(y == tick + 1, mine, weights), tick + 1) if tick + 1 < ticks else weights
        q, v, s, before, total = project(valid, sums, x, weights)
        prefix = arriving
        if tick + 1 < ticks:
            state = (prefix.astype(jnp.float32) + total).astype(jnp.bfloat16)
            arriving = lax.ppermute(state, "y", [(i, i + 1) for i in range(segments - 1)])
        x, own = mix(valid, own, x, weights, following, q, v, s, before, prefix)
        if tick + 1 < ticks:
            weights = following

    def part(flip):
        place = ((xh * groups + group) ^ flip) * count
        rows = lax.dynamic_slice_in_dim(x, place, count, 0)
        route = [(i, i ^ flip) for i in range(2 * groups)]
        return lax.ppermute(rows, ("xh", "xl", "core"), route) if flip else rows

    return join(group, [part(0), part(1), part(2), part(7)]).reshape(1, 1, count, groups * features)


def solution(mesh):
    split = Mesh(mesh.devices.reshape(4, 2, 2, 2, 8), ("y", "xh", "xl", "core", "z"))
    ctx = ("y", "xh", "xl", "core")
    placed = (P(None, ctx, None), P("z", None, None, None), P("z", None), P("z", None))
    return jax.shard_map(
        shards, mesh=split, in_specs=placed, out_specs=P("z", None, ctx, None), check_vma=False
    )
```

```python
import jax
import jax.numpy as jnp
from jax import lax
from jax.experimental import pallas as pl
from jax.experimental.pallas import tpu as pltpu
from jax.sharding import Mesh, PartitionSpec as P

EPS = 1e-06
B = 128
GAINS = 16


def prepare_kernel(info_ref, w_ref, gin_ref, gout_ref, out_ref):
    heads = w_ref.shape[0]
    for h in range(heads):
        out_ref[h * B : (h + 1) * B, :] = w_ref[h]
    rest = jnp.concatenate([gout_ref[0], gin_ref[0], jnp.zeros((GAINS - 2 * heads, B), jnp.float32)], 0)
    for part in range(3):
        piece = rest.astype(jnp.bfloat16)
        out_ref[heads * B :, part * B : (part + 1) * B] = piece
        rest = rest - piece.astype(jnp.float32)


def prepare(group, groups, w_qkv, norm_gain, out_gain):
    heads = w_qkv.shape[0] // groups

    def pick(i, info):
        return (info[0], 0, 0)

    return pl.pallas_call(
        prepare_kernel,
        grid_spec=pltpu.PrefetchScalarGridSpec(
            num_scalar_prefetch=1,
            grid=(1,),
            in_specs=[
                pl.BlockSpec((heads, B, 3 * B), pick),
                pl.BlockSpec((1, heads, B), pick),
                pl.BlockSpec((1, heads, B), pick),
            ],
            out_specs=pl.BlockSpec((heads * B + GAINS, 3 * B), lambda i, info: (0, 0)),
        ),
        out_shape=jax.ShapeDtypeStruct((heads * B + GAINS, 3 * B), jnp.bfloat16),
        name="prepare",
    )(group.reshape(1), w_qkv, norm_gain.reshape(groups, heads, B), out_gain.reshape(groups, heads, B))


def spread_kernel(x_ref, out_ref):
    copies, _, width = out_ref.shape
    for i in range(copies):
        lane = i * width % x_ref.shape[1]
        out_ref[i] = x_ref[:, lane : lane + width]


def spread(block, copies, width):
    return pl.pallas_call(
        spread_kernel,
        out_shape=jax.ShapeDtypeStruct((copies, block.shape[0], width), block.dtype),
        name="spread",
    )(block)


def join_kernel(parts_ref, out_ref):
    for g in range(parts_ref.shape[0]):
        width = parts_ref.shape[2]
        out_ref[:, g * width : (g + 1) * width] = parts_ref[g]


def join(parts):
    groups, rows, width = parts.shape
    return pl.pallas_call(
        join_kernel,
        out_shape=jax.ShapeDtypeStruct((rows, width * groups), parts.dtype),
        name="join",
    )(parts)


def mm(a, b, contract=(1, 0)):
    return lax.dot_general(a, b, (((contract[0],), (contract[1],)), ((), ())), preferred_element_type=jnp.float32)


def gains_of(w_ref, heads):
    parts = w_ref[heads * B :, :].astype(jnp.float32)
    return parts[:, :B] + parts[:, B : 2 * B] + parts[:, 2 * B :]


def project_kernel(info_ref, sums_ref, x_ref, w_ref, q_ref, v_ref, s_ref, before_ref, total_ref, r_ref, k_ref):
    tokens, features = x_ref.shape
    chunks = tokens // B
    heads = features // B

    @pl.when(info_ref[0] == 1)
    def _():
        r = lax.rsqrt(sums_ref[...] * (1.0 / 2048) + EPS)
        for c in range(chunks):
            r_ref[c * B : (c + 1) * B, :] = jnp.transpose(jnp.broadcast_to(r[c : c + 1, :], (B, B)))
        causal = lax.broadcasted_iota(jnp.int32, (B, B), 0) >= lax.broadcasted_iota(jnp.int32, (B, B), 1)
        gains = gains_of(w_ref, heads)
        for h in range(heads):
            lanes = slice(h * B, (h + 1) * B)
            gain_in = gains[heads + h : heads + h + 1]
            normed = (x_ref[:, lanes].astype(jnp.float32) * r_ref[...] * gain_in).astype(jnp.bfloat16)
            qkv = mm(normed, w_ref[lanes, :])
            q_ref[:, lanes] = (qkv[:, :B] * B**-0.5).astype(jnp.bfloat16)
            k_ref[...] = qkv[:, B : 2 * B].astype(jnp.bfloat16)
            v_ref[:, lanes] = qkv[:, 2 * B :].astype(jnp.bfloat16)
            total = jnp.zeros((B, B), jnp.float32)
            for c in range(chunks):
                rows = slice(c * B, (c + 1) * B)
                scores = mm(q_ref[rows, lanes], k_ref[rows, :], (1, 1))
                s_ref[rows, lanes] = jnp.where(causal, scores, 0.0).astype(jnp.bfloat16)
                before_ref[h, c] = total
                total = total + mm(k_ref[rows, :], v_ref[rows, lanes], (0, 0))
            total_ref[h] = total


def mix_kernel(info_ref, own_ref, x_ref, w_ref, q_ref, v_ref, s_ref, before_ref, p_ref, xo_ref, so_ref):
    tokens, features = x_ref.shape
    chunks = tokens // B
    heads = features // B
    valid = info_ref[0] == 1

    @pl.when(jnp.logical_not(valid))
    def _():
        so_ref[...] = own_ref[...]

    @pl.when(valid)
    def _():
        gains = gains_of(w_ref, heads)
        for c in range(chunks):
            rows = slice(c * B, (c + 1) * B)
            squares = None
            for h in range(heads):
                lanes = slice(h * B, (h + 1) * B)
                prefix = (p_ref[h].astype(jnp.float32) + before_ref[h, c]).astype(jnp.bfloat16)
                y = mm(
                    jnp.concatenate([s_ref[rows, lanes], q_ref[rows, lanes]], 1),
                    jnp.concatenate([v_ref[rows, lanes], prefix], 0),
                )
                mean = jnp.sum(y * y, 1, keepdims=True) * (1.0 / B)
                old = x_ref[rows, lanes].astype(jnp.float32)
                new = (old + y * lax.rsqrt(mean + EPS) * gains[h : h + 1]).astype(jnp.bfloat16)
                xo_ref[rows, lanes] = new
                new = new.astype(jnp.float32)
                squares = new * new if squares is None else squares + new * new
            so_ref[c : c + 1, :] = jnp.sum(jnp.transpose(squares), 0, keepdims=True)


def project(valid, sums, x, weights):
    tokens, features = x.shape
    heads = features // B
    chunks = tokens // B
    whole = pl.BlockSpec(memory_space=pltpu.VMEM)
    wide = jax.ShapeDtypeStruct((tokens, features), jnp.bfloat16)
    return pl.pallas_call(
        project_kernel,
        in_specs=[pl.BlockSpec(memory_space=pltpu.SMEM)] + [whole] * 3,
        out_specs=[whole] * 5,
        out_shape=[
            wide, wide, wide,
            jax.ShapeDtypeStruct((heads, chunks, B, B), jnp.float32),
            jax.ShapeDtypeStruct((heads, B, B), jnp.float32),
        ],
        scratch_shapes=[pltpu.VMEM((tokens, B), jnp.float32), pltpu.VMEM((tokens, B), jnp.bfloat16)],
        compiler_params=pltpu.CompilerParams(vmem_limit_bytes=8 * 1024 * 1024),
        cost_estimate=pl.CostEstimate(
            flops=tokens * features * 2 * 5 * B * 4, bytes_accessed=tokens * features, transcendentals=0
        ),
        name="project",
    )(valid, sums, x, weights)


def mix(valid, own, x, weights, q, v, s, before, prefix):
    tokens, features = x.shape
    whole = pl.BlockSpec(memory_space=pltpu.VMEM)
    return pl.pallas_call(
        mix_kernel,
        in_specs=[pl.BlockSpec(memory_space=pltpu.SMEM)] + [whole] * 8,
        out_specs=[whole] * 2,
        out_shape=[
            jax.ShapeDtypeStruct((tokens, features), jnp.bfloat16),
            jax.ShapeDtypeStruct((tokens // B, B), jnp.float32),
        ],
        input_output_aliases={2: 0},
        compiler_params=pltpu.CompilerParams(vmem_limit_bytes=8 * 1024 * 1024),
        cost_estimate=pl.CostEstimate(
            flops=tokens * features * 2 * 4 * B * 4, bytes_accessed=tokens * features, transcendentals=0
        ),
        name="mix",
    )(valid, own, x, weights, q, v, s, before, prefix)


def swap(block, axis):
    return lax.ppermute(block, axis, [(0, 1), (1, 0)])


def shards(tokens, w_qkv, norm_gain, out_gain):
    layers = lax.axis_size("z")
    segments = lax.axis_size("y")
    y, xh, xl, core, z = (lax.axis_index(a) for a in ("y", "xh", "xl", "core", "z"))
    line = ("xh", "xl", "core")
    groups = lax.axis_size(line)
    heads = w_qkv.shape[1] // groups
    features = heads * B
    group = (xh * lax.axis_size("xl") + xl) * lax.axis_size("core") + core

    mine = prepare(group, groups, w_qkv[0], norm_gain, out_gain)
    rows = range(segments)

    def rotate(held, step):
        going = [row for row in rows if 0 <= step - row < layers]
        route = [(row * layers + a, row * layers + (a - 1) % layers) for row in going for a in range(layers)]
        return lax.ppermute(held, ("y", "z"), route)

    weights = rotate(mine, 0)

    block = tokens[0]
    count = block.shape[0]
    table = spread(block, groups, features)
    x = lax.all_to_all(table, line, 0, 0, tiled=True)
    x = x.reshape(-1, features)
    wide = x.astype(jnp.float32)
    sums = jnp.sum(wide * wide, 1).reshape(-1, B)
    arriving = jnp.zeros((heads, B, B), jnp.bfloat16)

    own = sums
    ticks = layers + segments - 1
    for tick in range(ticks):
        step = tick - y + 1
        valid = ((step >= layers - z) & (step <= layers)).astype(jnp.int32).reshape(1)
        sums = own + swap(own, "core")
        sums = sums + swap(sums, "xl")
        sums = sums + lax.ppermute(sums, ("xh", "xl"), [(i, 3 - i) for i in range(4)])
        if tick + 1 < ticks:
            held = jnp.where(y == tick + 1, mine, weights)
            following = rotate(held, tick + 1)
        q, v, s, before, total = project(valid, sums, x, weights)
        prefix = arriving
        if tick + 1 < ticks:
            state = (prefix.astype(jnp.float32) + total).astype(jnp.bfloat16)
            arriving = lax.ppermute(state, "y", [(i, i + 1) for i in range(segments - 1)])
        x, own = mix(valid, own, x, weights, q, v, s, before, prefix)
        if tick + 1 < ticks:
            weights = following

    out = lax.all_to_all(x.reshape(groups, count, features), line, 0, 0, tiled=True)
    return join(out).reshape(1, 1, count, groups * features)


def solution(mesh):
    split = Mesh(mesh.devices.reshape(4, 2, 2, 2, 8), ("y", "xh", "xl", "core", "z"))
    ctx = ("y", "xh", "xl", "core")
    placed = (P(None, ctx, None), P("z", None, None, None), P("z", None), P("z", None))
    return jax.shard_map(
        shards, mesh=split, in_specs=placed, out_specs=P("z", None, ctx, None), check_vma=False
    )
```

```python
import jax
import jax.numpy as jnp
from jax import lax
from jax.experimental import pallas as pl
from jax.experimental.pallas import tpu as pltpu
from jax.sharding import Mesh, PartitionSpec as P

EPS = 1e-06
B = 128
GAINS = 16


def prepare_kernel(info_ref, w_ref, gin_ref, gout_ref, out_ref):
    heads = w_ref.shape[0]
    for h in range(heads):
        out_ref[h * B : (h + 1) * B, :] = w_ref[h]
    rest = jnp.concatenate([gout_ref[0], gin_ref[0], jnp.zeros((GAINS - 2 * heads, B), jnp.float32)], 0)
    for part in range(3):
        piece = rest.astype(jnp.bfloat16)
        out_ref[heads * B :, part * B : (part + 1) * B] = piece
        rest = rest - piece.astype(jnp.float32)


def prepare(group, groups, w_qkv, norm_gain, out_gain):
    heads = w_qkv.shape[0] // groups

    def pick(i, info):
        return (info[0], 0, 0)

    return pl.pallas_call(
        prepare_kernel,
        grid_spec=pltpu.PrefetchScalarGridSpec(
            num_scalar_prefetch=1,
            grid=(1,),
            in_specs=[
                pl.BlockSpec((heads, B, 3 * B), pick),
                pl.BlockSpec((1, heads, B), pick),
                pl.BlockSpec((1, heads, B), pick),
            ],
            out_specs=pl.BlockSpec((heads * B + GAINS, 3 * B), lambda i, info: (0, 0)),
        ),
        out_shape=jax.ShapeDtypeStruct((heads * B + GAINS, 3 * B), jnp.bfloat16),
        name="prepare",
    )(group.reshape(1), w_qkv, norm_gain.reshape(groups, heads, B), out_gain.reshape(groups, heads, B))


def spread_kernel(x_ref, out_ref):
    copies, _, width = out_ref.shape
    for i in range(copies):
        lane = i * width % x_ref.shape[1]
        out_ref[i] = x_ref[:, lane : lane + width]


def spread(block, copies, width):
    return pl.pallas_call(
        spread_kernel,
        out_shape=jax.ShapeDtypeStruct((copies, block.shape[0], width), block.dtype),
        name="spread",
    )(block)


def mm(a, b, contract=(1, 0)):
    return lax.dot_general(a, b, (((contract[0],), (contract[1],)), ((), ())), preferred_element_type=jnp.float32)


def gains_of(w_ref, heads):
    parts = w_ref[heads * B :, :].astype(jnp.float32)
    return parts[:, :B] + parts[:, B : 2 * B] + parts[:, 2 * B :]


def project_kernel(info_ref, sums_ref, x_ref, w_ref, q_ref, v_ref, s_ref, before_ref, total_ref, r_ref, k_ref):
    tokens, features = x_ref.shape
    chunks = tokens // B
    heads = features // B

    @pl.when(info_ref[0] == 1)
    def _():
        r = lax.rsqrt(sums_ref[...] * (1.0 / 2048) + EPS)
        for c in range(chunks):
            r_ref[c * B : (c + 1) * B, :] = jnp.transpose(jnp.broadcast_to(r[c : c + 1, :], (B, B)))
        causal = lax.broadcasted_iota(jnp.int32, (B, B), 0) >= lax.broadcasted_iota(jnp.int32, (B, B), 1)
        gains = gains_of(w_ref, heads)
        for h in range(heads):
            lanes = slice(h * B, (h + 1) * B)
            gain_in = gains[heads + h : heads + h + 1]
            normed = (x_ref[:, lanes].astype(jnp.float32) * r_ref[...] * gain_in).astype(jnp.bfloat16)
            qkv = mm(normed, w_ref[lanes, :])
            q_ref[:, lanes] = (qkv[:, :B] * B**-0.5).astype(jnp.bfloat16)
            k_ref[...] = qkv[:, B : 2 * B].astype(jnp.bfloat16)
            v_ref[:, lanes] = qkv[:, 2 * B :].astype(jnp.bfloat16)
            total = jnp.zeros((B, B), jnp.float32)
            for c in range(chunks):
                rows = slice(c * B, (c + 1) * B)
                scores = mm(q_ref[rows, lanes], k_ref[rows, :], (1, 1))
                s_ref[rows, lanes] = jnp.where(causal, scores, 0.0).astype(jnp.bfloat16)
                before_ref[h, c] = total
                total = total + mm(k_ref[rows, :], v_ref[rows, lanes], (0, 0))
            total_ref[h] = total


def mix_kernel(info_ref, own_ref, x_ref, w_ref, q_ref, v_ref, s_ref, before_ref, p_ref, xo_ref, so_ref):
    tokens, features = x_ref.shape
    chunks = tokens // B
    heads = features // B
    valid = info_ref[0] == 1

    @pl.when(jnp.logical_not(valid))
    def _():
        so_ref[...] = own_ref[...]

    @pl.when(valid)
    def _():
        gains = gains_of(w_ref, heads)
        for c in range(chunks):
            rows = slice(c * B, (c + 1) * B)
            squares = None
            for h in range(heads):
                lanes = slice(h * B, (h + 1) * B)
                prefix = (p_ref[h].astype(jnp.float32) + before_ref[h, c]).astype(jnp.bfloat16)
                y = mm(
                    jnp.concatenate([s_ref[rows, lanes], q_ref[rows, lanes]], 1),
                    jnp.concatenate([v_ref[rows, lanes], prefix], 0),
                )
                mean = jnp.sum(y * y, 1, keepdims=True) * (1.0 / B)
                old = x_ref[rows, lanes].astype(jnp.float32)
                new = (old + y * lax.rsqrt(mean + EPS) * gains[h : h + 1]).astype(jnp.bfloat16)
                xo_ref[rows, lanes] = new
                new = new.astype(jnp.float32)
                squares = new * new if squares is None else squares + new * new
            so_ref[c : c + 1, :] = jnp.sum(jnp.transpose(squares), 0, keepdims=True)


def project(valid, sums, x, weights):
    tokens, features = x.shape
    heads = features // B
    chunks = tokens // B
    whole = pl.BlockSpec(memory_space=pltpu.VMEM)
    wide = jax.ShapeDtypeStruct((tokens, features), jnp.bfloat16)
    return pl.pallas_call(
        project_kernel,
        in_specs=[pl.BlockSpec(memory_space=pltpu.SMEM)] + [whole] * 3,
        out_specs=[whole] * 5,
        out_shape=[
            wide, wide, wide,
            jax.ShapeDtypeStruct((heads, chunks, B, B), jnp.float32),
            jax.ShapeDtypeStruct((heads, B, B), jnp.float32),
        ],
        scratch_shapes=[pltpu.VMEM((tokens, B), jnp.float32), pltpu.VMEM((tokens, B), jnp.bfloat16)],
        compiler_params=pltpu.CompilerParams(vmem_limit_bytes=8 * 1024 * 1024),
        cost_estimate=pl.CostEstimate(
            flops=tokens * features * 2 * 5 * B * 4, bytes_accessed=tokens * features, transcendentals=0
        ),
        name="project",
    )(valid, sums, x, weights)


def mix(valid, own, x, weights, q, v, s, before, prefix):
    tokens, features = x.shape
    whole = pl.BlockSpec(memory_space=pltpu.VMEM)
    return pl.pallas_call(
        mix_kernel,
        in_specs=[pl.BlockSpec(memory_space=pltpu.SMEM)] + [whole] * 8,
        out_specs=[whole] * 2,
        out_shape=[
            jax.ShapeDtypeStruct((tokens, features), jnp.bfloat16),
            jax.ShapeDtypeStruct((tokens // B, B), jnp.float32),
        ],
        input_output_aliases={2: 0},
        compiler_params=pltpu.CompilerParams(vmem_limit_bytes=8 * 1024 * 1024),
        cost_estimate=pl.CostEstimate(
            flops=tokens * features * 2 * 4 * B * 4, bytes_accessed=tokens * features, transcendentals=0
        ),
        name="mix",
    )(valid, own, x, weights, q, v, s, before, prefix)


def swap(block, axis):
    return lax.ppermute(block, axis, [(0, 1), (1, 0)])


def shards(tokens, w_qkv, norm_gain, out_gain):
    layers = lax.axis_size("z")
    segments = lax.axis_size("y")
    y, xh, xl, core, z = (lax.axis_index(a) for a in ("y", "xh", "xl", "core", "z"))
    line = ("xh", "xl", "core")
    groups = lax.axis_size(line)
    heads = w_qkv.shape[1] // groups
    features = heads * B
    group = (xh * lax.axis_size("xl") + xl) * lax.axis_size("core") + core

    mine = prepare(group, groups, w_qkv[0], norm_gain, out_gain)
    rows = range(segments)

    def rotate(held, step):
        going = [row for row in rows if 0 <= step - row < layers - 1]
        if not going:
            return held
        route = [(row * layers + a, row * layers + (a - 1) % layers) for row in going for a in range(layers)]
        return lax.ppermute(held, ("y", "z"), route)

    weights = rotate(mine, 0)
    following = rotate(jnp.where(y == 1, mine, weights), 1)

    block = tokens[0]
    count = block.shape[0]
    table = spread(block, groups, features)
    x = lax.all_to_all(table, line, 0, 0, tiled=True)
    x = x.reshape(-1, features)
    wide = x.astype(jnp.float32)
    sums = jnp.sum(wide * wide, 1).reshape(-1, B)
    arriving = jnp.zeros((heads, B, B), jnp.bfloat16)

    own = sums
    ticks = layers + segments - 1
    for tick in range(ticks):
        step = tick - y + 1
        valid = ((step >= layers - z) & (step <= layers)).astype(jnp.int32).reshape(1)
        sums = own + swap(own, "core")
        sums = jnp.where(following[0, 0] > 2, 0.0, sums)
        sums = sums + swap(sums, "xl")
        sums = sums + lax.ppermute(sums, ("xh", "xl"), [(i, 3 - i) for i in range(4)])
        later = rotate(jnp.where((y == tick + 2) | (sums[0, 0] < 0), mine, following), tick + 2)
        if tick + 1 >= layers:
            weights = jnp.where(y == tick + 1 - layers, mine, weights)
        q, v, s, before, total = project(valid, sums, x, weights)
        prefix = arriving
        if tick + 1 < ticks:
            state = (prefix.astype(jnp.float32) + total).astype(jnp.bfloat16)
            arriving = lax.ppermute(state, "y", [(i, i + 1) for i in range(segments - 1)])
        x, own = mix(valid, own, x, weights, q, v, s, before, prefix)
        weights, following = following, later

    out = lax.all_to_all(x.reshape(groups, count, features), line, 0, 0, tiled=True)
    return jnp.transpose(out, (1, 0, 2)).reshape(1, 1, count, groups * features)


def solution(mesh):
    split = Mesh(mesh.devices.reshape(4, 2, 2, 2, 8), ("y", "xh", "xl", "core", "z"))
    ctx = ("y", "xh", "xl", "core")
    placed = (P(None, ctx, None), P("z", None, None, None), P("z", None), P("z", None))
    return jax.shard_map(
        shards, mesh=split, in_specs=placed, out_specs=P("z", None, ctx, None), check_vma=False
    )
```

```python
import jax
import jax.numpy as jnp
from jax import lax
from jax.experimental import pallas as pl
from jax.experimental.pallas import tpu as pltpu
from jax.sharding import Mesh, PartitionSpec as P

EPS = 1e-06
B = 128
GAINS = 16


def prepare_kernel(info_ref, w_ref, gin_ref, gout_ref, out_ref):
    heads = w_ref.shape[0]
    for h in range(heads):
        out_ref[h * B : (h + 1) * B, :] = w_ref[h]
    rest = jnp.concatenate([gout_ref[0], gin_ref[0], jnp.zeros((GAINS - 2 * heads, B), jnp.float32)], 0)
    for part in range(3):
        piece = rest.astype(jnp.bfloat16)
        out_ref[heads * B :, part * B : (part + 1) * B] = piece
        rest = rest - piece.astype(jnp.float32)


def prepare(group, groups, w_qkv, norm_gain, out_gain):
    heads = w_qkv.shape[0] // groups

    def pick(i, info):
        return (info[0], 0, 0)

    return pl.pallas_call(
        prepare_kernel,
        grid_spec=pltpu.PrefetchScalarGridSpec(
            num_scalar_prefetch=1,
            grid=(1,),
            in_specs=[
                pl.BlockSpec((heads, B, 3 * B), pick),
                pl.BlockSpec((1, heads, B), pick),
                pl.BlockSpec((1, heads, B), pick),
            ],
            out_specs=pl.BlockSpec((heads * B + GAINS, 3 * B), lambda i, info: (0, 0)),
        ),
        out_shape=jax.ShapeDtypeStruct((heads * B + GAINS, 3 * B), jnp.bfloat16),
        name="prepare",
    )(group.reshape(1), w_qkv, norm_gain.reshape(groups, heads, B), out_gain.reshape(groups, heads, B))


def spread_kernel(x_ref, out_ref):
    copies, _, width = out_ref.shape
    for i in range(copies):
        lane = i * width % x_ref.shape[1]
        out_ref[i] = x_ref[:, lane : lane + width]


def spread(block, copies, width):
    return pl.pallas_call(
        spread_kernel,
        out_shape=jax.ShapeDtypeStruct((copies, block.shape[0], width), block.dtype),
        name="spread",
    )(block)


def mm(a, b, contract=(1, 0)):
    return lax.dot_general(a, b, (((contract[0],), (contract[1],)), ((), ())), preferred_element_type=jnp.float32)


def gains_of(w_ref, heads):
    parts = w_ref[heads * B :, :].astype(jnp.float32)
    return parts[:, :B] + parts[:, B : 2 * B] + parts[:, 2 * B :]


def project_kernel(info_ref, sums_ref, x_ref, w_ref, q_ref, v_ref, s_ref, before_ref, total_ref, r_ref, k_ref):
    tokens, features = x_ref.shape
    chunks = tokens // B
    heads = features // B

    @pl.when(info_ref[0] == 1)
    def _():
        r = lax.rsqrt(sums_ref[...] * (1.0 / 2048) + EPS)
        for c in range(chunks):
            r_ref[c * B : (c + 1) * B, :] = jnp.transpose(jnp.broadcast_to(r[c : c + 1, :], (B, B)))
        causal = lax.broadcasted_iota(jnp.int32, (B, B), 0) >= lax.broadcasted_iota(jnp.int32, (B, B), 1)
        gains = gains_of(w_ref, heads)
        for h in range(heads):
            lanes = slice(h * B, (h + 1) * B)
            gain_in = gains[heads + h : heads + h + 1]
            normed = (x_ref[:, lanes].astype(jnp.float32) * r_ref[...] * gain_in).astype(jnp.bfloat16)
            qkv = mm(normed, w_ref[lanes, :])
            q_ref[:, lanes] = (qkv[:, :B] * B**-0.5).astype(jnp.bfloat16)
            k_ref[...] = qkv[:, B : 2 * B].astype(jnp.bfloat16)
            v_ref[:, lanes] = qkv[:, 2 * B :].astype(jnp.bfloat16)
            total = jnp.zeros((B, B), jnp.float32)
            for c in range(chunks):
                rows = slice(c * B, (c + 1) * B)
                scores = mm(q_ref[rows, lanes], k_ref[rows, :], (1, 1))
                s_ref[rows, lanes] = jnp.where(causal, scores, 0.0).astype(jnp.bfloat16)
                before_ref[h, c] = total
                total = total + mm(k_ref[rows, :], v_ref[rows, lanes], (0, 0))
            total_ref[h] = total


def mix_kernel(info_ref, own_ref, x_ref, w_ref, q_ref, v_ref, s_ref, before_ref, p_ref, xo_ref, so_ref):
    tokens, features = x_ref.shape
    chunks = tokens // B
    heads = features // B
    valid = info_ref[0] == 1

    @pl.when(jnp.logical_not(valid))
    def _():
        so_ref[...] = own_ref[...]

    @pl.when(valid)
    def _():
        gains = gains_of(w_ref, heads)
        for c in range(chunks):
            rows = slice(c * B, (c + 1) * B)
            squares = None
            for h in range(heads):
                lanes = slice(h * B, (h + 1) * B)
                prefix = (p_ref[h].astype(jnp.float32) + before_ref[h, c]).astype(jnp.bfloat16)
                y = mm(
                    jnp.concatenate([s_ref[rows, lanes], q_ref[rows, lanes]], 1),
                    jnp.concatenate([v_ref[rows, lanes], prefix], 0),
                )
                mean = jnp.sum(y * y, 1, keepdims=True) * (1.0 / B)
                old = x_ref[rows, lanes].astype(jnp.float32)
                new = (old + y * lax.rsqrt(mean + EPS) * gains[h : h + 1]).astype(jnp.bfloat16)
                xo_ref[rows, lanes] = new
                new = new.astype(jnp.float32)
                squares = new * new if squares is None else squares + new * new
            so_ref[c : c + 1, :] = jnp.sum(jnp.transpose(squares), 0, keepdims=True)


def project(valid, sums, x, weights):
    tokens, features = x.shape
    heads = features // B
    chunks = tokens // B
    whole = pl.BlockSpec(memory_space=pltpu.VMEM)
    wide = jax.ShapeDtypeStruct((tokens, features), jnp.bfloat16)
    return pl.pallas_call(
        project_kernel,
        in_specs=[pl.BlockSpec(memory_space=pltpu.SMEM)] + [whole] * 3,
        out_specs=[whole] * 5,
        out_shape=[
            wide, wide, wide,
            jax.ShapeDtypeStruct((heads, chunks, B, B), jnp.float32),
            jax.ShapeDtypeStruct((heads, B, B), jnp.float32),
        ],
        scratch_shapes=[pltpu.VMEM((tokens, B), jnp.float32), pltpu.VMEM((tokens, B), jnp.bfloat16)],
        compiler_params=pltpu.CompilerParams(vmem_limit_bytes=8 * 1024 * 1024),
        cost_estimate=pl.CostEstimate(
            flops=tokens * features * 2 * 5 * B * 4, bytes_accessed=tokens * features, transcendentals=0
        ),
        name="project",
    )(valid, sums, x, weights)


def mix(valid, own, x, weights, q, v, s, before, prefix):
    tokens, features = x.shape
    whole = pl.BlockSpec(memory_space=pltpu.VMEM)
    return pl.pallas_call(
        mix_kernel,
        in_specs=[pl.BlockSpec(memory_space=pltpu.SMEM)] + [whole] * 8,
        out_specs=[whole] * 2,
        out_shape=[
            jax.ShapeDtypeStruct((tokens, features), jnp.bfloat16),
            jax.ShapeDtypeStruct((tokens // B, B), jnp.float32),
        ],
        input_output_aliases={2: 0},
        compiler_params=pltpu.CompilerParams(vmem_limit_bytes=8 * 1024 * 1024),
        cost_estimate=pl.CostEstimate(
            flops=tokens * features * 2 * 4 * B * 4, bytes_accessed=tokens * features, transcendentals=0
        ),
        name="mix",
    )(valid, own, x, weights, q, v, s, before, prefix)


def swap(block, axis):
    return lax.ppermute(block, axis, [(0, 1), (1, 0)])


def shards(tokens, w_qkv, norm_gain, out_gain):
    layers = lax.axis_size("z")
    segments = lax.axis_size("y")
    y, xh, xl, core, z = (lax.axis_index(a) for a in ("y", "xh", "xl", "core", "z"))
    groups = lax.axis_size("xl") * lax.axis_size("core")
    heads = w_qkv.shape[1] // groups
    features = heads * B
    group = xl * lax.axis_size("core") + core

    mine = prepare(group, groups, w_qkv[0], norm_gain, out_gain)
    rows = range(segments)

    def rotate(held, step):
        going = [row for row in rows if 0 <= step - row < layers - 1]
        if not going:
            return held
        route = [(row * layers + a, row * layers + (a - 1) % layers) for row in going for a in range(layers)]
        return lax.ppermute(held, ("y", "z"), route)

    weights = rotate(mine, 0)

    block = tokens[0]
    count = block.shape[0]
    table = spread(block, 2 * groups, features)
    x = lax.all_to_all(table, ("xh", "xl", "core"), 0, 0, tiled=True)
    x = x.reshape(-1, features)
    wide = x.astype(jnp.float32)
    sums = jnp.sum(wide * wide, 1).reshape(-1, B)
    arriving = jnp.zeros((heads, B, B), jnp.bfloat16)

    own = sums
    ticks = layers + segments - 1
    for tick in range(ticks):
        step = tick - y + 1
        valid = ((step >= layers - z) & (step <= layers)).astype(jnp.int32).reshape(1)
        sums = own + swap(own, "core")
        sums = sums + swap(sums, "xl")
        following = rotate(jnp.where(y == tick + 1, mine, weights), tick + 1)
        if tick + 1 >= layers:
            weights = jnp.where(y == tick + 1 - layers, mine, weights)
        q, v, s, before, total = project(valid, sums, x, weights)
        prefix = arriving
        if tick + 1 < ticks:
            state = (prefix.astype(jnp.float32) + total).astype(jnp.bfloat16)
            arriving = lax.ppermute(state, "y", [(i, i + 1) for i in range(segments - 1)])
        x, own = mix(valid, own, x, weights, q, v, s, before, prefix)
        weights = following

    def part(flip):
        place = ((xh * groups + group) ^ flip) * count
        rows = lax.dynamic_slice_in_dim(x, place, count, 0)
        route = [(i, i ^ flip) for i in range(2 * groups)]
        return lax.ppermute(rows, ("xh", "xl", "core"), route) if flip else rows

    parts = [part(0), part(1), part(2), part(7)]
    out = []
    for g in range(groups):
        near, far = (jnp.where(core == g % 2, *parts[i : i + 2]) for i in (0, 2))
        out.append(jnp.where(xl == g // 2, near, far))
    return jnp.concatenate(out, 1).reshape(1, 1, count, groups * features)


def solution(mesh):
    split = Mesh(mesh.devices.reshape(4, 2, 2, 2, 8), ("y", "xh", "xl", "core", "z"))
    ctx = ("y", "xh", "xl", "core")
    placed = (P(None, ctx, None), P("z", None, None, None), P("z", None), P("z", None))
    return jax.shard_map(
        shards, mesh=split, in_specs=placed, out_specs=P("z", None, ctx, None), check_vma=False
    )
```

```python
import jax
import jax.numpy as jnp
from jax import lax
from jax.experimental import pallas as pl
from jax.experimental.pallas import tpu as pltpu
from jax.sharding import Mesh, PartitionSpec as P

EPS = 1e-06
B = 128
GAINS = 16


def prepare_kernel(info_ref, w_ref, gin_ref, gout_ref, out_ref):
    heads = w_ref.shape[0]
    for h in range(heads):
        out_ref[h * B : (h + 1) * B, :] = w_ref[h]
    rest = jnp.concatenate([gout_ref[0], gin_ref[0], jnp.zeros((GAINS - 2 * heads, B), jnp.float32)], 0)
    for part in range(3):
        piece = rest.astype(jnp.bfloat16)
        out_ref[heads * B :, part * B : (part + 1) * B] = piece
        rest = rest - piece.astype(jnp.float32)


def prepare(group, groups, w_qkv, norm_gain, out_gain):
    heads = w_qkv.shape[0] // groups

    def pick(i, info):
        return (info[0], 0, 0)

    return pl.pallas_call(
        prepare_kernel,
        grid_spec=pltpu.PrefetchScalarGridSpec(
            num_scalar_prefetch=1,
            grid=(1,),
            in_specs=[
                pl.BlockSpec((heads, B, 3 * B), pick),
                pl.BlockSpec((1, heads, B), pick),
                pl.BlockSpec((1, heads, B), pick),
            ],
            out_specs=pl.BlockSpec((heads * B + GAINS, 3 * B), lambda i, info: (0, 0)),
        ),
        out_shape=jax.ShapeDtypeStruct((heads * B + GAINS, 3 * B), jnp.bfloat16),
        name="prepare",
    )(group.reshape(1), w_qkv, norm_gain.reshape(groups, heads, B), out_gain.reshape(groups, heads, B))


def spread_kernel(x_ref, out_ref):
    copies, _, width = out_ref.shape
    for i in range(copies):
        lane = i * width % x_ref.shape[1]
        out_ref[i] = x_ref[:, lane : lane + width]


def spread(block, copies, width):
    return pl.pallas_call(
        spread_kernel,
        out_shape=jax.ShapeDtypeStruct((copies, block.shape[0], width), block.dtype),
        name="spread",
    )(block)


def mm(a, b, contract=(1, 0)):
    return lax.dot_general(a, b, (((contract[0],), (contract[1],)), ((), ())), preferred_element_type=jnp.float32)


def gains_of(w_ref, heads):
    parts = w_ref[heads * B :, :].astype(jnp.float32)
    return parts[:, :B] + parts[:, B : 2 * B] + parts[:, 2 * B :]


def project_kernel(info_ref, sums_ref, x_ref, w_ref, q_ref, v_ref, s_ref, before_ref, total_ref, r_ref, k_ref):
    tokens, features = x_ref.shape
    chunks = tokens // B
    heads = features // B

    @pl.when(info_ref[0] == 1)
    def _():
        r = lax.rsqrt(sums_ref[...] * (1.0 / 2048) + EPS)
        for c in range(chunks):
            r_ref[c * B : (c + 1) * B, :] = jnp.transpose(jnp.broadcast_to(r[c : c + 1, :], (B, B)))
        causal = lax.broadcasted_iota(jnp.int32, (B, B), 0) >= lax.broadcasted_iota(jnp.int32, (B, B), 1)
        gains = gains_of(w_ref, heads)
        for h in range(heads):
            lanes = slice(h * B, (h + 1) * B)
            gain_in = gains[heads + h : heads + h + 1]
            normed = (x_ref[:, lanes].astype(jnp.float32) * r_ref[...] * gain_in).astype(jnp.bfloat16)
            qkv = mm(normed, w_ref[lanes, :])
            q_ref[:, lanes] = (qkv[:, :B] * B**-0.5).astype(jnp.bfloat16)
            k_ref[...] = qkv[:, B : 2 * B].astype(jnp.bfloat16)
            v_ref[:, lanes] = qkv[:, 2 * B :].astype(jnp.bfloat16)
            total = jnp.zeros((B, B), jnp.float32)
            for c in range(chunks):
                rows = slice(c * B, (c + 1) * B)
                scores = mm(q_ref[rows, lanes], k_ref[rows, :], (1, 1))
                s_ref[rows, lanes] = jnp.where(causal, scores, 0.0).astype(jnp.bfloat16)
                before_ref[h, c] = total
                total = total + mm(k_ref[rows, :], v_ref[rows, lanes], (0, 0))
            total_ref[h] = total


def mix_kernel(info_ref, own_ref, x_ref, w_ref, q_ref, v_ref, s_ref, before_ref, p_ref, xo_ref, so_ref):
    tokens, features = x_ref.shape
    chunks = tokens // B
    heads = features // B
    valid = info_ref[0] == 1

    @pl.when(jnp.logical_not(valid))
    def _():
        so_ref[...] = own_ref[...]

    @pl.when(valid)
    def _():
        gains = gains_of(w_ref, heads)
        for c in range(chunks):
            rows = slice(c * B, (c + 1) * B)
            squares = None
            for h in range(heads):
                lanes = slice(h * B, (h + 1) * B)
                prefix = (p_ref[h].astype(jnp.float32) + before_ref[h, c]).astype(jnp.bfloat16)
                y = mm(
                    jnp.concatenate([s_ref[rows, lanes], q_ref[rows, lanes]], 1),
                    jnp.concatenate([v_ref[rows, lanes], prefix], 0),
                )
                mean = jnp.sum(y * y, 1, keepdims=True) * (1.0 / B)
                old = x_ref[rows, lanes].astype(jnp.float32)
                new = (old + y * lax.rsqrt(mean + EPS) * gains[h : h + 1]).astype(jnp.bfloat16)
                xo_ref[rows, lanes] = new
                new = new.astype(jnp.float32)
                squares = new * new if squares is None else squares + new * new
            so_ref[c : c + 1, :] = jnp.sum(jnp.transpose(squares), 0, keepdims=True)


def project(valid, sums, x, weights):
    tokens, features = x.shape
    heads = features // B
    chunks = tokens // B
    whole = pl.BlockSpec(memory_space=pltpu.VMEM)
    wide = jax.ShapeDtypeStruct((tokens, features), jnp.bfloat16)
    return pl.pallas_call(
        project_kernel,
        in_specs=[pl.BlockSpec(memory_space=pltpu.SMEM)] + [whole] * 3,
        out_specs=[whole] * 5,
        out_shape=[
            wide, wide, wide,
            jax.ShapeDtypeStruct((heads, chunks, B, B), jnp.float32),
            jax.ShapeDtypeStruct((heads, B, B), jnp.float32),
        ],
        scratch_shapes=[pltpu.VMEM((tokens, B), jnp.float32), pltpu.VMEM((tokens, B), jnp.bfloat16)],
        compiler_params=pltpu.CompilerParams(vmem_limit_bytes=8 * 1024 * 1024),
        cost_estimate=pl.CostEstimate(
            flops=tokens * features * 2 * 5 * B * 4, bytes_accessed=tokens * features, transcendentals=0
        ),
        name="project",
    )(valid, sums, x, weights)


def mix(valid, own, x, weights, q, v, s, before, prefix):
    tokens, features = x.shape
    whole = pl.BlockSpec(memory_space=pltpu.VMEM)
    return pl.pallas_call(
        mix_kernel,
        in_specs=[pl.BlockSpec(memory_space=pltpu.SMEM)] + [whole] * 8,
        out_specs=[whole] * 2,
        out_shape=[
            jax.ShapeDtypeStruct((tokens, features), jnp.bfloat16),
            jax.ShapeDtypeStruct((tokens // B, B), jnp.float32),
        ],
        input_output_aliases={2: 0},
        compiler_params=pltpu.CompilerParams(vmem_limit_bytes=8 * 1024 * 1024),
        cost_estimate=pl.CostEstimate(
            flops=tokens * features * 2 * 4 * B * 4, bytes_accessed=tokens * features, transcendentals=0
        ),
        name="mix",
    )(valid, own, x, weights, q, v, s, before, prefix)


def swap(block, axis):
    return lax.ppermute(block, axis, [(0, 1), (1, 0)])


def shards(tokens, w_qkv, norm_gain, out_gain):
    layers = lax.axis_size("z")
    segments = lax.axis_size("y")
    y, xh, xl, core, z = (lax.axis_index(a) for a in ("y", "xh", "xl", "core", "z"))
    groups = lax.axis_size("xl") * lax.axis_size("core")
    heads = w_qkv.shape[1] // groups
    features = heads * B
    group = xl * lax.axis_size("core") + core

    mine = prepare(group, groups, w_qkv[0], norm_gain, out_gain)
    rows = range(segments)

    def rotate(held, step):
        going = [row for row in rows if 0 <= step - row < layers - 1]
        if not going:
            return held
        route = [(row * layers + a, row * layers + (a - 1) % layers) for row in going for a in range(layers)]
        return lax.ppermute(held, ("y", "z"), route)

    weights = rotate(mine, 0)

    block = tokens[0]
    count = block.shape[0]
    table = spread(block, 2 * groups, features)
    x = lax.all_to_all(table, ("xh", "xl", "core"), 0, 0, tiled=True)
    x = x.reshape(-1, features)
    wide = x.astype(jnp.float32)
    sums = jnp.sum(wide * wide, 1).reshape(-1, B)
    arriving = jnp.zeros((heads, B, B), jnp.bfloat16)

    own = sums
    ticks = layers + segments - 1
    for tick in range(ticks):
        step = tick - y + 1
        valid = ((step >= layers - z) & (step <= layers)).astype(jnp.int32).reshape(1)
        first = own + swap(own, "core")
        sums = jnp.where(weights[:8, :B] > 2, 0.0, first) + swap(first, "xl")
        following = rotate(jnp.where(y == tick + 1, mine, weights), tick + 1)
        if tick + 1 >= layers:
            weights = jnp.where(y == tick + 1 - layers, mine, weights)
        q, v, s, before, total = project(valid, sums, x, weights)
        prefix = arriving
        if tick + 1 < ticks:
            state = (prefix.astype(jnp.float32) + total).astype(jnp.bfloat16)
            arriving = lax.ppermute(state, "y", [(i, i + 1) for i in range(segments - 1)])
        x, own = mix(valid, own, x, weights, q, v, s, before, prefix)
        weights = following

    def part(flip):
        place = ((xh * groups + group) ^ flip) * count
        rows = lax.dynamic_slice_in_dim(x, place, count, 0)
        route = [(i, i ^ flip) for i in range(2 * groups)]
        return lax.ppermute(rows, ("xh", "xl", "core"), route) if flip else rows

    parts = [part(0), part(1), part(2), part(7)]
    out = []
    for g in range(groups):
        near, far = (jnp.where(core == g % 2, *parts[i : i + 2]) for i in (0, 2))
        out.append(jnp.where(xl == g // 2, near, far))
    return jnp.concatenate(out, 1).reshape(1, 1, count, groups * features)


def solution(mesh):
    split = Mesh(mesh.devices.reshape(4, 2, 2, 2, 8), ("y", "xh", "xl", "core", "z"))
    ctx = ("y", "xh", "xl", "core")
    placed = (P(None, ctx, None), P("z", None, None, None), P("z", None), P("z", None))
    return jax.shard_map(
        shards, mesh=split, in_specs=placed, out_specs=P("z", None, ctx, None), check_vma=False
    )
```

```python
import jax
import jax.numpy as jnp
from jax import lax
from jax.experimental import pallas as pl
from jax.experimental.pallas import tpu as pltpu
from jax.sharding import Mesh, PartitionSpec as P

EPS = 1e-06
B = 128
GAINS = 16


def prepare_kernel(info_ref, w_ref, gin_ref, gout_ref, out_ref):
    heads = w_ref.shape[0]
    for h in range(heads):
        out_ref[h * B : (h + 1) * B, :] = w_ref[h]
    rest = jnp.concatenate([gout_ref[0], gin_ref[0], jnp.zeros((GAINS - 2 * heads, B), jnp.float32)], 0)
    for part in range(3):
        piece = rest.astype(jnp.bfloat16)
        out_ref[heads * B :, part * B : (part + 1) * B] = piece
        rest = rest - piece.astype(jnp.float32)


def prepare(group, groups, w_qkv, norm_gain, out_gain):
    heads = w_qkv.shape[0] // groups

    def pick(i, info):
        return (info[0], 0, 0)

    return pl.pallas_call(
        prepare_kernel,
        grid_spec=pltpu.PrefetchScalarGridSpec(
            num_scalar_prefetch=1,
            grid=(1,),
            in_specs=[
                pl.BlockSpec((heads, B, 3 * B), pick),
                pl.BlockSpec((1, heads, B), pick),
                pl.BlockSpec((1, heads, B), pick),
            ],
            out_specs=pl.BlockSpec((heads * B + GAINS, 3 * B), lambda i, info: (0, 0)),
        ),
        out_shape=jax.ShapeDtypeStruct((heads * B + GAINS, 3 * B), jnp.bfloat16),
        name="prepare",
    )(group.reshape(1), w_qkv, norm_gain.reshape(groups, heads, B), out_gain.reshape(groups, heads, B))


def spread_kernel(x_ref, out_ref):
    copies, _, width = out_ref.shape
    for i in range(copies):
        lane = i * width % x_ref.shape[1]
        out_ref[i] = x_ref[:, lane : lane + width]


def spread(block, copies, width):
    return pl.pallas_call(
        spread_kernel,
        out_shape=jax.ShapeDtypeStruct((copies, block.shape[0], width), block.dtype),
        name="spread",
    )(block)


def mm(a, b, contract=(1, 0)):
    return lax.dot_general(a, b, (((contract[0],), (contract[1],)), ((), ())), preferred_element_type=jnp.float32)


def gains_of(w_ref, heads):
    parts = w_ref[heads // 2 * B :, :].astype(jnp.float32)
    return parts[:, :B] + parts[:, B : 2 * B] + parts[:, 2 * B :]


def project_kernel(info_ref, sums_ref, x_ref, first_ref, w_ref, q_ref, v_ref, s_ref, before_ref, total_ref, r_ref, k_ref):
    tokens, features = x_ref.shape
    chunks = tokens // B
    heads = features // B

    @pl.when(info_ref[0] == 1)
    def _():
        r = lax.rsqrt(sums_ref[...] * (1.0 / 2048) + EPS)
        for c in range(chunks):
            r_ref[c * B : (c + 1) * B, :] = jnp.transpose(jnp.broadcast_to(r[c : c + 1, :], (B, B)))
        causal = lax.broadcasted_iota(jnp.int32, (B, B), 0) >= lax.broadcasted_iota(jnp.int32, (B, B), 1)
        gains = gains_of(w_ref, heads)
        split = first_ref.shape[0] // B
        for h in range(heads):
            maps = first_ref if h < split else w_ref
            place = h % split * B
            lanes = slice(h * B, (h + 1) * B)
            gain_in = gains[heads + h : heads + h + 1]
            normed = (x_ref[:, lanes].astype(jnp.float32) * r_ref[...] * gain_in).astype(jnp.bfloat16)
            qkv = mm(normed, maps[place : place + B, :])
            q_ref[:, lanes] = (qkv[:, :B] * B**-0.5).astype(jnp.bfloat16)
            k_ref[...] = qkv[:, B : 2 * B].astype(jnp.bfloat16)
            v_ref[:, lanes] = qkv[:, 2 * B :].astype(jnp.bfloat16)
            total = jnp.zeros((B, B), jnp.float32)
            for c in range(chunks):
                rows = slice(c * B, (c + 1) * B)
                scores = mm(q_ref[rows, lanes], k_ref[rows, :], (1, 1))
                s_ref[rows, lanes] = jnp.where(causal, scores, 0.0).astype(jnp.bfloat16)
                before_ref[h, c] = total
                total = total + mm(k_ref[rows, :], v_ref[rows, lanes], (0, 0))
            total_ref[h] = total


def mix_kernel(info_ref, own_ref, x_ref, w_ref, q_ref, v_ref, s_ref, before_ref, p_ref, xo_ref, so_ref):
    tokens, features = x_ref.shape
    chunks = tokens // B
    heads = features // B
    valid = info_ref[0] == 1

    @pl.when(jnp.logical_not(valid))
    def _():
        so_ref[...] = own_ref[...]

    @pl.when(valid)
    def _():
        gains = gains_of(w_ref, heads)
        for c in range(chunks):
            rows = slice(c * B, (c + 1) * B)
            squares = None
            for h in range(heads):
                lanes = slice(h * B, (h + 1) * B)
                prefix = (p_ref[h].astype(jnp.float32) + before_ref[h, c]).astype(jnp.bfloat16)
                y = mm(
                    jnp.concatenate([s_ref[rows, lanes], q_ref[rows, lanes]], 1),
                    jnp.concatenate([v_ref[rows, lanes], prefix], 0),
                )
                mean = jnp.sum(y * y, 1, keepdims=True) * (1.0 / B)
                old = x_ref[rows, lanes].astype(jnp.float32)
                new = (old + y * lax.rsqrt(mean + EPS) * gains[h : h + 1]).astype(jnp.bfloat16)
                xo_ref[rows, lanes] = new
                new = new.astype(jnp.float32)
                squares = new * new if squares is None else squares + new * new
            so_ref[c : c + 1, :] = jnp.sum(jnp.transpose(squares), 0, keepdims=True)


def project(valid, sums, x, weights):
    tokens, features = x.shape
    heads = features // B
    chunks = tokens // B
    whole = pl.BlockSpec(memory_space=pltpu.VMEM)
    wide = jax.ShapeDtypeStruct((tokens, features), jnp.bfloat16)
    return pl.pallas_call(
        project_kernel,
        in_specs=[pl.BlockSpec(memory_space=pltpu.SMEM)] + [whole] * 4,
        out_specs=[whole] * 5,
        out_shape=[
            wide, wide, wide,
            jax.ShapeDtypeStruct((heads, chunks, B, B), jnp.float32),
            jax.ShapeDtypeStruct((heads, B, B), jnp.float32),
        ],
        scratch_shapes=[pltpu.VMEM((tokens, B), jnp.float32), pltpu.VMEM((tokens, B), jnp.bfloat16)],
        compiler_params=pltpu.CompilerParams(vmem_limit_bytes=8 * 1024 * 1024),
        cost_estimate=pl.CostEstimate(
            flops=tokens * features * 2 * 5 * B * 4, bytes_accessed=tokens * features, transcendentals=0
        ),
        name="project",
    )(valid, sums, x, *weights)


def mix(valid, own, x, weights, q, v, s, before, prefix):
    tokens, features = x.shape
    whole = pl.BlockSpec(memory_space=pltpu.VMEM)
    return pl.pallas_call(
        mix_kernel,
        in_specs=[pl.BlockSpec(memory_space=pltpu.SMEM)] + [whole] * 8,
        out_specs=[whole] * 2,
        out_shape=[
            jax.ShapeDtypeStruct((tokens, features), jnp.bfloat16),
            jax.ShapeDtypeStruct((tokens // B, B), jnp.float32),
        ],
        input_output_aliases={2: 0},
        compiler_params=pltpu.CompilerParams(vmem_limit_bytes=8 * 1024 * 1024),
        cost_estimate=pl.CostEstimate(
            flops=tokens * features * 2 * 4 * B * 4, bytes_accessed=tokens * features, transcendentals=0
        ),
        name="mix",
    )(valid, own, x, weights[1], q, v, s, before, prefix)


def swap(block, axis):
    return lax.ppermute(block, axis, [(0, 1), (1, 0)])


def shards(tokens, w_qkv, norm_gain, out_gain):
    layers = lax.axis_size("z")
    segments = lax.axis_size("y")
    y, xh, xl, core, z = (lax.axis_index(a) for a in ("y", "xh", "xl", "core", "z"))
    groups = lax.axis_size("xl") * lax.axis_size("core")
    heads = w_qkv.shape[1] // groups
    features = heads * B
    group = xl * lax.axis_size("core") + core

    mine = prepare(group, groups, w_qkv[0], norm_gain, out_gain)
    mine = (mine[: features // 2], mine[features // 2 :])

    def choose(own_row, held):
        return tuple(jnp.where(y == own_row, a, b) for a, b in zip(mine, held))

    rows = range(segments)

    def rotate(held, step):
        going = [row for row in rows if 0 <= step - row < layers - 1]
        if not going:
            return held
        route = [(row * layers + a, row * layers + (a - 1) % layers) for row in going for a in range(layers)]
        return tuple(lax.ppermute(part, ("y", "z"), route) for part in held)

    weights = rotate(mine, 0)

    block = tokens[0]
    count = block.shape[0]
    table = spread(block, 2 * groups, features)
    x = lax.all_to_all(table, ("xh", "xl", "core"), 0, 0, tiled=True)
    x = x.reshape(-1, features)
    wide = x.astype(jnp.float32)
    sums = jnp.sum(wide * wide, 1).reshape(-1, B)
    arriving = jnp.zeros((heads, B, B), jnp.bfloat16)

    own = sums
    ticks = layers + segments - 1
    for tick in range(ticks):
        step = tick - y + 1
        valid = ((step >= layers - z) & (step <= layers)).astype(jnp.int32).reshape(1)
        first = own + swap(own, "core")
        sums = jnp.where((weights[0][:8, :B] > 2) | (weights[1][:8, :B] > 2), 0.0, first) + swap(first, "xl")
        following = rotate(choose(tick + 1, weights), tick + 1)
        if tick + 1 >= layers:
            weights = choose(tick + 1 - layers, weights)
        q, v, s, before, total = project(valid, sums, x, weights)
        prefix = arriving
        if tick + 1 < ticks:
            state = (prefix.astype(jnp.float32) + total).astype(jnp.bfloat16)
            arriving = lax.ppermute(state, "y", [(i, i + 1) for i in range(segments - 1)])
        x, own = mix(valid, own, x, weights, q, v, s, before, prefix)
        weights = following

    def part(flip):
        place = ((xh * groups + group) ^ flip) * count
        rows = lax.dynamic_slice_in_dim(x, place, count, 0)
        route = [(i, i ^ flip) for i in range(2 * groups)]
        return lax.ppermute(rows, ("xh", "xl", "core"), route) if flip else rows

    parts = [part(0), part(1), part(2), part(7)]
    out = []
    for g in range(groups):
        near, far = (jnp.where(core == g % 2, *parts[i : i + 2]) for i in (0, 2))
        out.append(jnp.where(xl == g // 2, near, far))
    return jnp.concatenate(out, 1).reshape(1, 1, count, groups * features)


def solution(mesh):
    split = Mesh(mesh.devices.reshape(4, 2, 2, 2, 8), ("y", "xh", "xl", "core", "z"))
    ctx = ("y", "xh", "xl", "core")
    placed = (P(None, ctx, None), P("z", None, None, None), P("z", None), P("z", None))
    return jax.shard_map(
        shards, mesh=split, in_specs=placed, out_specs=P("z", None, ctx, None), check_vma=False
    )
```

```python
import jax
import jax.numpy as jnp
from jax import lax
from jax.experimental import pallas as pl
from jax.experimental.pallas import tpu as pltpu
from jax.sharding import Mesh, PartitionSpec as P

EPS = 1e-06
B = 128
GAINS = 16


def prepare_kernel(info_ref, w_ref, gin_ref, gout_ref, out_ref):
    heads = w_ref.shape[0]
    for h in range(heads):
        out_ref[h * B : (h + 1) * B, :] = w_ref[h]
    rest = jnp.concatenate([gout_ref[0], gin_ref[0], jnp.zeros((GAINS - 2 * heads, B), jnp.float32)], 0)
    for part in range(3):
        piece = rest.astype(jnp.bfloat16)
        out_ref[heads * B :, part * B : (part + 1) * B] = piece
        rest = rest - piece.astype(jnp.float32)


def prepare(group, groups, w_qkv, norm_gain, out_gain):
    heads = w_qkv.shape[0] // groups

    def pick(i, info):
        return (info[0], 0, 0)

    return pl.pallas_call(
        prepare_kernel,
        grid_spec=pltpu.PrefetchScalarGridSpec(
            num_scalar_prefetch=1,
            grid=(1,),
            in_specs=[
                pl.BlockSpec((heads, B, 3 * B), pick),
                pl.BlockSpec((1, heads, B), pick),
                pl.BlockSpec((1, heads, B), pick),
            ],
            out_specs=pl.BlockSpec((heads * B + GAINS, 3 * B), lambda i, info: (0, 0)),
        ),
        out_shape=jax.ShapeDtypeStruct((heads * B + GAINS, 3 * B), jnp.bfloat16),
        name="prepare",
    )(group.reshape(1), w_qkv, norm_gain.reshape(groups, heads, B), out_gain.reshape(groups, heads, B))


def spread_kernel(x_ref, out_ref):
    copies, _, width = out_ref.shape
    for i in range(copies):
        lane = i * width % x_ref.shape[1]
        out_ref[i] = x_ref[:, lane : lane + width]


def spread(block, copies, width):
    return pl.pallas_call(
        spread_kernel,
        out_shape=jax.ShapeDtypeStruct((copies, block.shape[0], width), block.dtype),
        name="spread",
    )(block)


def mm(a, b, contract=(1, 0)):
    return lax.dot_general(a, b, (((contract[0],), (contract[1],)), ((), ())), preferred_element_type=jnp.float32)


def gains_of(w_ref, heads):
    parts = w_ref[heads * B :, :].astype(jnp.float32)
    return parts[:, :B] + parts[:, B : 2 * B] + parts[:, 2 * B :]


def project_kernel(info_ref, sums_ref, x_ref, w_ref, q_ref, v_ref, s_ref, before_ref, total_ref, r_ref, k_ref):
    tokens, features = x_ref.shape
    chunks = tokens // B
    heads = features // B

    @pl.when(info_ref[0] == 1)
    def _():
        r = lax.rsqrt(sums_ref[...] * (1.0 / 2048) + EPS)
        for c in range(chunks):
            r_ref[c * B : (c + 1) * B, :] = jnp.transpose(jnp.broadcast_to(r[c : c + 1, :], (B, B)))
        causal = lax.broadcasted_iota(jnp.int32, (B, B), 0) >= lax.broadcasted_iota(jnp.int32, (B, B), 1)
        gains = gains_of(w_ref, heads)
        for h in range(heads):
            lanes = slice(h * B, (h + 1) * B)
            gain_in = gains[heads + h : heads + h + 1]
            normed = (x_ref[:, lanes].astype(jnp.float32) * r_ref[...] * gain_in).astype(jnp.bfloat16)
            qkv = mm(normed, w_ref[lanes, :])
            q_ref[:, lanes] = (qkv[:, :B] * B**-0.5).astype(jnp.bfloat16)
            k_ref[...] = qkv[:, B : 2 * B].astype(jnp.bfloat16)
            v_ref[:, lanes] = qkv[:, 2 * B :].astype(jnp.bfloat16)
            total = jnp.zeros((B, B), jnp.float32)
            for c in range(chunks):
                rows = slice(c * B, (c + 1) * B)
                scores = mm(q_ref[rows, lanes], k_ref[rows, :], (1, 1))
                s_ref[rows, lanes] = jnp.where(causal, scores, 0.0).astype(jnp.bfloat16)
                before_ref[h, c] = total
                total = total + mm(k_ref[rows, :], v_ref[rows, lanes], (0, 0))
            total_ref[h] = total


def mix_kernel(info_ref, own_ref, x_ref, w_ref, q_ref, v_ref, s_ref, before_ref, p_ref, xo_ref, so_ref):
    tokens, features = x_ref.shape
    chunks = tokens // B
    heads = features // B
    valid = info_ref[0] == 1

    @pl.when(jnp.logical_not(valid))
    def _():
        so_ref[...] = own_ref[...]

    @pl.when(valid)
    def _():
        gains = gains_of(w_ref, heads)
        for c in range(chunks):
            rows = slice(c * B, (c + 1) * B)
            squares = None
            for h in range(heads):
                lanes = slice(h * B, (h + 1) * B)
                prefix = (p_ref[h].astype(jnp.float32) + before_ref[h, c]).astype(jnp.bfloat16)
                y = mm(
                    jnp.concatenate([s_ref[rows, lanes], q_ref[rows, lanes]], 1),
                    jnp.concatenate([v_ref[rows, lanes], prefix], 0),
                )
                mean = jnp.sum(y * y, 1, keepdims=True) * (1.0 / B)
                old = x_ref[rows, lanes].astype(jnp.float32)
                new = (old + y * lax.rsqrt(mean + EPS) * gains[h : h + 1]).astype(jnp.bfloat16)
                xo_ref[rows, lanes] = new
                new = new.astype(jnp.float32)
                squares = new * new if squares is None else squares + new * new
            so_ref[c : c + 1, :] = jnp.sum(jnp.transpose(squares), 0, keepdims=True)


def project(valid, sums, x, weights):
    tokens, features = x.shape
    heads = features // B
    chunks = tokens // B
    whole = pl.BlockSpec(memory_space=pltpu.VMEM)
    wide = jax.ShapeDtypeStruct((tokens, features), jnp.bfloat16)
    return pl.pallas_call(
        project_kernel,
        in_specs=[pl.BlockSpec(memory_space=pltpu.SMEM)] + [whole] * 3,
        out_specs=[whole] * 5,
        out_shape=[
            wide, wide, wide,
            jax.ShapeDtypeStruct((heads, chunks, B, B), jnp.float32),
            jax.ShapeDtypeStruct((heads, B, B), jnp.float32),
        ],
        scratch_shapes=[pltpu.VMEM((tokens, B), jnp.float32), pltpu.VMEM((tokens, B), jnp.bfloat16)],
        compiler_params=pltpu.CompilerParams(vmem_limit_bytes=8 * 1024 * 1024),
        cost_estimate=pl.CostEstimate(
            flops=tokens * features * 2 * 5 * B * 4, bytes_accessed=tokens * features, transcendentals=0
        ),
        name="project",
    )(valid, sums, x, weights)


def mix(valid, own, x, weights, q, v, s, before, prefix):
    tokens, features = x.shape
    whole = pl.BlockSpec(memory_space=pltpu.VMEM)
    return pl.pallas_call(
        mix_kernel,
        in_specs=[pl.BlockSpec(memory_space=pltpu.SMEM)] + [whole] * 8,
        out_specs=[whole] * 2,
        out_shape=[
            jax.ShapeDtypeStruct((tokens, features), jnp.bfloat16),
            jax.ShapeDtypeStruct((tokens // B, B), jnp.float32),
        ],
        input_output_aliases={2: 0},
        compiler_params=pltpu.CompilerParams(vmem_limit_bytes=8 * 1024 * 1024),
        cost_estimate=pl.CostEstimate(
            flops=tokens * features * 2 * 4 * B * 4, bytes_accessed=tokens * features, transcendentals=0
        ),
        name="mix",
    )(valid, own, x, weights, q, v, s, before, prefix)


def swap(block, axis):
    return lax.ppermute(block, axis, [(0, 1), (1, 0)])


def shards(tokens, w_qkv, norm_gain, out_gain):
    layers = lax.axis_size("z")
    segments = lax.axis_size("y")
    y, xh, xl, core, z = (lax.axis_index(a) for a in ("y", "xh", "xl", "core", "z"))
    groups = lax.axis_size("xl") * lax.axis_size("core")
    heads = w_qkv.shape[1] // groups
    features = heads * B
    group = xl * lax.axis_size("core") + core

    mine = prepare(group, groups, w_qkv[0], norm_gain, out_gain)
    rows = range(segments)

    def rotate(held, step):
        going = [row for row in rows if 0 <= step - row < layers - 1]
        if not going:
            return held
        route = [
            (row * layers + a, row * layers + (a - 1) % layers)
            for row in going
            for a in range(layers)
            if (a + step - row) % layers != layers - 1
        ]
        return lax.ppermute(held, ("y", "z"), route)

    weights = rotate(mine, 0)

    block = tokens[0]
    count = block.shape[0]
    table = spread(block, 2 * groups, features)
    x = lax.all_to_all(table, ("xh", "xl", "core"), 0, 0, tiled=True)
    x = x.reshape(-1, features)
    wide = x.astype(jnp.float32)
    sums = jnp.sum(wide * wide, 1).reshape(-1, B)
    arriving = jnp.zeros((heads, B, B), jnp.bfloat16)

    own = sums
    ticks = layers + segments - 1
    for tick in range(ticks):
        step = tick - y + 1
        valid = ((step >= layers - z) & (step <= layers)).astype(jnp.int32).reshape(1)
        first = own + swap(own, "core")
        sums = jnp.where(weights[:8, :B] > 2, 0.0, first) + swap(first, "xl")
        following = rotate(jnp.where(y == tick + 1, mine, weights), tick + 1)
        if tick + 1 >= layers:
            weights = jnp.where(y == tick + 1 - layers, mine, weights)
        q, v, s, before, total = project(valid, sums, x, weights)
        prefix = arriving
        if tick + 1 < ticks:
            state = (prefix.astype(jnp.float32) + total).astype(jnp.bfloat16)
            arriving = lax.ppermute(state, "y", [(i, i + 1) for i in range(segments - 1)])
        x, own = mix(valid, own, x, weights, q, v, s, before, prefix)
        weights = following

    def part(flip):
        place = ((xh * groups + group) ^ flip) * count
        rows = lax.dynamic_slice_in_dim(x, place, count, 0)
        route = [(i, i ^ flip) for i in range(2 * groups)]
        return lax.ppermute(rows, ("xh", "xl", "core"), route) if flip else rows

    parts = [part(0), part(1), part(2), part(7)]
    out = []
    for g in range(groups):
        near, far = (jnp.where(core == g % 2, *parts[i : i + 2]) for i in (0, 2))
        out.append(jnp.where(xl == g // 2, near, far))
    return jnp.concatenate(out, 1).reshape(1, 1, count, groups * features)


def solution(mesh):
    split = Mesh(mesh.devices.reshape(4, 2, 2, 2, 8), ("y", "xh", "xl", "core", "z"))
    ctx = ("y", "xh", "xl", "core")
    placed = (P(None, ctx, None), P("z", None, None, None), P("z", None), P("z", None))
    return jax.shard_map(
        shards, mesh=split, in_specs=placed, out_specs=P("z", None, ctx, None), check_vma=False
    )
```
